512 devices in a mesh: dp: 32 (over y, x), tensor: 16 (over z, core).
Axes of the slice: x: 4, y: 8, z: 8, core: 2. Of those that a mesh axis runs over, the one named last changes fastest.
Arguments:
- hidden_acts: bfloat16 [8192, 53248], P('dp', 'tensor'), parts along dimension 0, may hold values from -6 to 6
- mixing: float32 [52, 52], replicated, may hold values from -0.875 to 0.875
- packed_codes: int32 [53248, 256], P('tensor'), may hold values from 0 to 65535, as said below
- exponents: int32 [1024], replicated, may hold values from -1 to 1
Outputs:
- projected: bfloat16 [8192, 1024], P('dp', 'tensor'), parts along dimension 0
The draws below stay inside these ranges and needn't reach their ends.
There are 32 independent parts, one for each index of `dp`. The reference program is written for one: setup_inputs(seed, part) draws one part's arguments, and reference() takes and returns one part's arrays. A program takes and returns all parts, laid end to end along the dimension named above; an argument that names none is the same for every part. Nothing has to cross between parts.
Inputs may be any that keep to these rules, and one draw needn't show every extreme that they name: `packed_codes`: each word holds four independent 4-bit fields in its low 16 bits, each uniform over its 16 patterns; the higher bits are zero.
All inputs are finite; a program needn't handle non-finite values.
Results may differ from the reference program's by a relative error of at most 0.015.
Values may be sent and summed in bfloat16 or wider, within the bound.
A program may use at most 64 MiB of HBM per device.

```python
import jax
import jax.numpy as jnp
from jax import lax

OUTER = 16
INNER_H = 64
INNER_M = 52
FF = 53248
OUT = 1024
ROWS = 256


def draw_packed_codes(key, part):
    key = jax.random.fold_in(key, 7)
    fields = jax.random.randint(key, (FF, OUT // 4, 4), 0, 16, dtype=jnp.int32)
    fields = fields.at[0, 0, :].set(15)
    fields = fields.at[0, 1, :].set(0)
    word = jnp.zeros((FF, OUT // 4), jnp.int32)
    for k in range(4):
        word = jnp.bitwise_or(word, jnp.left_shift(fields[:, :, k], 4 * k))
    return word


def plant(values, key, least, top_value):
    extent = values.shape
    index_at = [jax.random.randint(jax.random.fold_in(key, axis), (), 0, extent[axis]) for axis in range(len(extent))]
    values = values.at[tuple(index_at)].set(least)
    longest = extent.index(max(extent))
    index_at[longest] = (index_at[longest] + 1) % extent[longest]
    return values.at[tuple(index_at)].set(top_value)


def level_of(stream_key, extent, cuts, low, high):
    def one(axis_at, shards_of):
        draws = jax.random.uniform(jax.random.fold_in(jax.random.fold_in(stream_key, 6), axis_at), (shards_of,), jnp.float32, low / len(cuts), high / len(cuts))
        return jnp.repeat(jnp.exp(draws), extent[axis_at] // shards_of).reshape((-1,) + (1,) * (len(extent) - axis_at - 1))

    loudness = one(*cuts[0])
    for cut in cuts[1:]:
        loudness = loudness * one(*cut)
    return loudness


def noise(rng, dims, width, bound, split=(), held_as=jnp.bfloat16):
    entries = width * jax.random.normal(rng, dims, jnp.float32)
    if split:
        entries = entries * level_of(rng, dims, split, -0.22, 0.18)
    return jnp.clip(entries, -bound, bound).astype(held_as)


def setup_inputs(seed: int = 0, part: int = 0) -> dict:
    splits = jax.random.split(jax.random.key(seed), 5)
    part_keys = jax.random.split(jax.random.fold_in(splits[4], part), 5)
    return {
        "hidden_acts": noise(part_keys[0], (ROWS, FF), 1.0, 6.0, ((1, 16),)),
        "mixing": noise(splits[1], (INNER_M, INNER_M), INNER_M ** -0.5, 0.875, (), jnp.float32),
        "packed_codes": draw_packed_codes(jax.random.fold_in(splits[4], 71), part),
        "exponents": plant(jax.random.randint(splits[3], (OUT,), -1, 2), jax.random.fold_in(splits[3], 1), -1, 1).astype(jnp.int32),
    }


def sylvester(order):
    index = jnp.arange(order, dtype=jnp.int32)
    both = index[:, None] & index[None, :]
    parity = jnp.zeros((order, order), jnp.int32)
    for bit_pos in range(max(order.bit_length() - 1, 0)):
        parity = parity + ((both >> bit_pos) & 1)
    return (1 - 2 * (parity & 1)).astype(jnp.float32)


def reference(hidden_acts, mixing, packed_codes, exponents):
    blocks = hidden_acts.astype(jnp.float32).reshape(ROWS, OUTER, INNER_H, INNER_M)
    hadamard_inner = sylvester(INNER_H)
    hadamard_outer = sylvester(OUTER)
    mixed = jnp.einsum("race,eg->racg", blocks, mixing, precision=lax.Precision.HIGHEST)
    inner = (jnp.einsum("racg,cd->radg", mixed, hadamard_inner, precision=lax.Precision.HIGHEST) / 8.0).astype(jnp.bfloat16)
    rotated = jnp.einsum("radg,ab->rbdg", inner.astype(jnp.float32), hadamard_outer, precision=lax.Precision.HIGHEST) / 4.0
    rotated = rotated.astype(jnp.bfloat16).reshape(ROWS, FF)

    def one_field(shift_left):
        field = jnp.right_shift(jnp.left_shift(packed_codes, shift_left), 28)
        return jnp.dot(rotated, field.astype(jnp.bfloat16), preferred_element_type=jnp.float32)

    shifts = jnp.array([28 - 4 * k for k in range(4)], jnp.int32)
    parts = lax.map(one_field, shifts)
    acc = jnp.transpose(parts, (1, 0, 2)).reshape(ROWS, OUT)
    scale = jnp.exp2(exponents.astype(jnp.float32)) / 1024.0
    return (acc * scale[None, :]).astype(jnp.bfloat16)
```

```python
import jax
import jax.numpy as jnp
from jax import lax
from jax.experimental import pallas as pl
from jax.experimental.pallas import tpu as pltpu
from jax.sharding import PartitionSpec as P

MESH = pl.DeviceIdType.MESH
NY, NX, NT = 8, 4, 16
ROWS = 256
HALF = ROWS // 2
INNER_M = 52
QUARTER = 832
QPAD = 896
SLICE = 208
TILE = 16
TILES = SLICE // TILE
PIECES = ((0, 112), (112, 96))
F32, BF16 = jnp.float32, jnp.bfloat16


def iota(shape, dim):
    return lax.broadcasted_iota(jnp.int32, shape, dim)


def kernel(
    acts, mix, codes, expo, out,
    xbuf, cbuf, mpad, gbuf, zbuf, s1, r1, s2, wbuf, ins, inr, pk, ces, cer, xs, xr, zs, zr, fs, fr,
    lsem, s1s, s1r, s2s, s2r, us, ur, ds, dr, iss, irs, css, crs, xss, xrs, zss, zrs, fss, frs,
):
    dp = lax.axis_index("dp")
    t = lax.axis_index("tensor")
    y, x = dp // NX, dp % NX
    z, core = t // 2, t % 2
    sib = t + 1 - 2 * core
    fy, jy = y % 2, y // 2
    up = ((y + 1) % NY) * NX + x
    down = ((y + NY - 1) % NY) * NX + x

    def along_t(dest):
        return (dp, dest)

    def along_x(dest):
        return (y * NX + dest, t)

    def rcopy(src, dst, ssem, rsem, dev):
        return pltpu.make_async_remote_copy(
            src_ref=src, dst_ref=dst, send_sem=ssem, recv_sem=rsem, device_id=dev, device_id_type=MESH
        )

    barrier = pltpu.get_barrier_semaphore()

    def greet(dev):
        pl.semaphore_signal(barrier, inc=1, device_id=dev, device_id_type=MESH)

    @pl.loop(1, NT)
    def _(o):
        greet(along_t((t + o) % NT))

    @pl.loop(1, NX)
    def _(o):
        greet(along_x((x + o) % NX))

    greet((up, t))
    greet((down, t))

    row0 = pl.multiple_of(x * QUARTER + jy * SLICE, 16)
    get_codes = pltpu.make_async_copy(codes.at[pl.ds(row0, SLICE)], cbuf, lsem.at[0])
    get_codes.start()
    get_acts = pltpu.make_async_copy(acts, xbuf, lsem.at[1])
    get_acts.start()
    get_codes.wait()
    for h in range(2):
        shift = 28 - 4 * (h + 2 * fy)
        field = jnp.right_shift(jnp.left_shift(cbuf[...], shift), 28)
        s1[h] = field.astype(F32).astype(BF16).reshape(TILES, TILE, 256)
    pl.semaphore_wait(barrier, NT - 1 + NX - 1 + 2)

    def first(h, i):
        return rcopy(s1.at[h, i], r1.at[h, t], s1s.at[h, i], s1r.at[h, t], along_t(i + 3 * h))

    for h in range(2):

        @pl.loop(0, TILES)
        def _(o):
            i = (t + o) % TILES

            @pl.when(i + 3 * h != t)
            def _():
                first(h, i).start()

    mpad[...] = jnp.zeros_like(mpad)
    mpad[0:INNER_M, 0:INNER_M] = mix[...]

    def block_of(v):
        return jnp.right_shift(v * 1261, 16)

    both = jnp.bitwise_and(iota((128, 128), 0), iota((128, 128), 1))
    both = jnp.bitwise_xor(both, jnp.right_shift(both, 2))
    both = jnp.bitwise_xor(both, jnp.right_shift(both, 1))
    had = (1 - 2 * jnp.bitwise_and(both, 1)).astype(F32).astype(BF16)
    cols = iota((128, QPAD), 1)
    inside = cols < QUARTER
    cblock = block_of(cols)
    which = iota((128, QPAD), 0)
    col_block = jnp.where(inside & (cblock == which), 1.0, 0.0).astype(BF16)
    col_inner = jnp.where(inside & (cols - INNER_M * cblock == which), 1.0, 0.0).astype(BF16)
    mixing = mpad[...].astype(BF16)
    right_m = jnp.dot(mixing, col_inner, preferred_element_type=F32).astype(BF16)
    right_h = jnp.dot(had, col_block, preferred_element_type=F32).astype(BF16)

    @pl.loop(0, 4)
    def _(blk):
        at = pl.multiple_of(blk * 240, 16)
        rows = iota((240, 128), 0) + (at - 64)
        ok = (rows >= 0) & (rows < QUARTER)
        rblock = block_of(rows)
        lane = iota((240, 128), 1)
        row_block = jnp.where(ok & (rblock == lane), 1.0, 0.0).astype(BF16)
        row_inner = jnp.where(ok & (rows - INNER_M * rblock == lane), 1.0, 0.0).astype(BF16)
        m_part = jnp.dot(row_inner, right_m, preferred_element_type=F32)
        h_part = jnp.dot(row_block, right_h, preferred_element_type=F32)
        gbuf[pl.ds(at, 240)] = (m_part * h_part).astype(BF16)

    get_acts.wait()
    for q in range(4):
        lo = q * QUARTER - 64 * (q % 2)
        g = gbuf[0:QPAD] if q % 2 else gbuf[64 : 64 + QPAD]
        zbuf[q] = jnp.dot(xbuf[:, lo : lo + QPAD], g, preferred_element_type=F32)

    @pl.loop(0, ROWS // 16)
    def _(blk):
        rows = pl.ds(pl.multiple_of(blk * 16, 16), 16)
        z0, z1, z2, z3 = (zbuf[q, rows, :] for q in range(4))
        u0, u1, u2, u3 = z0 + z1, z0 - z1, z2 + z3, z2 - z3
        for q, v in enumerate((u0 + u2, u1 + u3, u0 - u2, u1 - u3)):
            ins[q, rows, :] = (v * 0.125).astype(BF16)

    def spread(q):
        return rcopy(ins.at[q], inr.at[x], iss.at[q], irs.at[x], along_x(q))

    for d in (2, 1, 3):
        spread((x + d) % NX).start()
    inr[x] = ins[x]

    def tile_at(h, i):
        return wbuf.at[h, fy, pl.ds(pl.multiple_of(jy * SLICE + i * TILE, 16), TILE)]

    def second(h, a):
        i = t - 3 * h
        return rcopy(s2.at[h, a], tile_at(h, i), s2s.at[h, a], s2r.at[h, i], along_t(a))

    def mine(h):
        i = t - 3 * h
        return (i >= 0) & (i < TILES)

    for f in range(2):
        for h in range(2):
            wbuf[h, f, QUARTER:QPAD, :] = jnp.zeros((QPAD - QUARTER, 256), BF16)

    for h in range(2):

        @pl.when(mine(h))
        def _():
            @pl.loop(1, NT)
            def _(o):
                b = (t + o) % NT
                rcopy(s1.at[h, 0], r1.at[h, b], s1s.at[h, 0], s1r.at[h, b], along_t(b)).wait_recv()

            r1[h, t] = s1[h, t - 3 * h]
            for half in range(2):
                lanes = slice(128 * half, 128 * half + 128)
                v = [r1[h, b, :, lanes].astype(F32) for b in range(NT)]
                for bit in (1, 2, 4, 8):
                    v = [v[a ^ bit] - v[a] if a & bit else v[a] + v[a ^ bit] for a in range(NT)]
                for a in range(NT):
                    s2[h, a, :, lanes] = v[a].astype(BF16)

            @pl.loop(1, NT)
            def _(o):
                second(h, (t + o) % NT).start()

            wbuf[h, fy, pl.ds(pl.multiple_of(jy * SLICE + (t - 3 * h) * TILE, 16), TILE), :] = s2[h, t]

    def assembled(h):
        @pl.loop(0, TILES)
        def _(i):
            @pl.when(i + 3 * h != t)
            def _():
                rcopy(s2.at[h, 0], tile_at(h, i), s2s.at[h, 0], s2r.at[h, i], along_t(i + 3 * h)).wait_recv()

    def ring(h, step, piece, sign):
        yy = (y - sign * step + NY) % NY
        off, size = PIECES[piece]
        part = wbuf.at[h, yy % 2, pl.ds(pl.multiple_of((yy // 2) * SLICE + off, 16), size)]
        if sign > 0:
            return rcopy(part, part, us.at[h, step, piece], ur.at[h, step, piece], (up, t))
        return rcopy(part, part, ds.at[h, step, piece], dr.at[h, step, piece], (down, t))

    def arrived(h, step, piece, sign):
        yy = (y - sign * (step + 1) + NY) % NY
        off, size = PIECES[piece]
        part = wbuf.at[h, yy % 2, pl.ds(pl.multiple_of((yy // 2) * SLICE + off, 16), size)]
        if sign > 0:
            rcopy(part, part, us.at[h, step, piece], ur.at[h, step, piece], (up, t)).wait_recv()
        else:
            rcopy(part, part, ds.at[h, step, piece], dr.at[h, step, piece], (down, t)).wait_recv()

    def ring_start(h):
        for piece in range(2):
            ring(h, 0, piece, 1).start()
            ring(h, 0, piece, -1).start()

    def ring_step(h, s):
        if s == 4:
            arrived(h, 3, 0, 1)
            arrived(h, 3, 1, -1)
            return
        for piece in range(2):
            arrived(h, s - 1, piece, 1)
            if s < 3 or piece == 0:
                ring(h, s, piece, 1).start()
            arrived(h, s - 1, piece, -1)
            if s < 3 or piece == 1:
                ring(h, s, piece, -1).start()

    def product(h, half_of):
        rows = pl.ds(pl.multiple_of(half_of * HALF, HALF), HALF)
        lhs = inr[:, rows, :].reshape(NX * HALF, QPAD)
        return [
            jnp.dot(lhs, wbuf[h, f], preferred_element_type=F32).reshape(NX, HALF, 256) for f in range(2)
        ]

    def swap_cores(h):
        return rcopy(ces.at[h], cer.at[h], css.at[h], crs.at[h], along_t(sib))

    def partials(h):
        for f, v in enumerate(product(h, 1 - core)):
            ces[h, :, :, 256 * f : 256 * f + 256] = v.astype(BF16)
        swap_cores(h).start()
        for f, v in enumerate(product(h, core)):
            pk[h, :, :, 256 * f : 256 * f + 256] = v

    def over_x(h, p):
        return rcopy(xs.at[h, p], xr.at[h, x], xss.at[h, p], xrs.at[h, x], along_x(p))

    def reduce_x(h):
        swap_cores(h).wait_recv()

        @pl.loop(0, NX)
        def _(p):
            v = pk[h, p] + cer[h, p].astype(F32)
            pk[h, p] = v
            xs[h, p] = v.astype(BF16)

        for d in (2, 1, 3):
            over_x(h, (x + d) % NX).start()

    def chip_of(h, i):
        return 2 * h + 4 * (i // 2) + i % 2

    def over_z(h, i):
        dest = 2 * chip_of(h, i) + core
        return rcopy(zs.at[h, i], zr.at[z], zss.at[h, i], zrs.at[z], along_t(dest))

    def reduce_z(h):
        for d in (1, 3, 2):
            src = (x + d) % NX
            rcopy(xs.at[h, 0], xr.at[h, src], xss.at[h, 0], xrs.at[h, src], along_x(src)).wait_recv()
        total = pk[h, x]
        for d in (1, 2, 3):
            total = total + xr[h, (x + d) % NX].astype(F32)
        for i in range(4):
            zs[h, i] = total[:, 128 * i : 128 * i + 128].astype(BF16)
        for i in range(4):

            @pl.when(chip_of(h, i) != z)
            def _():
                over_z(h, i).start()

            @pl.when(chip_of(h, i) == z)
            def _():
                fs[...] = total[:, 128 * i : 128 * i + 128]

    assembled(0)
    ring_start(0)
    ring_step(0, 1)
    ring_step(0, 2)
    assembled(1)
    ring_step(0, 3)
    ring_start(1)
    ring_step(0, 4)
    ring_step(1, 1)
    ring_step(1, 2)
    for d in (1, 3, 2):
        src = (x + d) % NX
        rcopy(ins.at[0], inr.at[src], iss.at[0], irs.at[src], along_x(src)).wait_recv()
    partials(0)
    ring_step(1, 3)
    reduce_x(0)
    ring_step(1, 4)
    partials(1)
    reduce_z(0)
    reduce_x(1)
    reduce_z(1)

    def total_of_z(o, acc):
        src = (z + o) % 8
        rcopy(zs.at[0, 0], zr.at[src], zss.at[0, 0], zrs.at[src], along_t(2 * src + core)).wait_recv()
        return acc + zr[src].astype(F32)

    total = lax.fori_loop(1, 8, total_of_z, fs[...])
    two = jnp.left_shift(jnp.ones((1, 128), jnp.int32), expo[pl.ds(z, 1), :] + 16)
    total = total * (two.astype(F32) * (2.0 ** -28))
    fs[...] = total
    last = rcopy(fs, fr, fss, frs, along_t(sib))
    last.start()

    def own_columns(v):
        return jnp.where(core == 1, v[:, 64:], v[:, :64]).astype(BF16)

    out[pl.ds(pl.multiple_of(core * HALF, HALF), HALF), :] = own_columns(total)
    last.wait_recv()
    out[pl.ds(pl.multiple_of((1 - core) * HALF, HALF), HALF), :] = own_columns(fr[...])

    last.wait_send()
    for h in range(2):

        @pl.loop(0, TILES)
        def _(i):
            @pl.when(i + 3 * h != t)
            def _():
                first(h, i).wait_send()

        @pl.when(mine(h))
        def _():
            @pl.loop(1, NT)
            def _(o):
                second(h, (t + o) % NT).wait_send()

        for s in range(4):
            for piece in range(2):
                if s < 3 or piece == 0:
                    ring(h, s, piece, 1).wait_send()
                if s < 3 or piece == 1:
                    ring(h, s, piece, -1).wait_send()
        swap_cores(h).wait_send()
        for d in (1, 2, 3):
            over_x(h, (x + d) % NX).wait_send()
        for i in range(4):

            @pl.when(chip_of(h, i) != z)
            def _():
                over_z(h, i).wait_send()

    for d in (1, 2, 3):
        spread((x + d) % NX).wait_send()


def per_device(hidden_acts, mixing, packed_codes, exponents):
    vmem = pltpu.VMEM
    dma = pltpu.SemaphoreType.DMA
    scratch = [
        vmem((ROWS, 3328), BF16),
        vmem((SLICE, 256), jnp.int32),
        vmem((128, 128), F32),
        vmem((QPAD + 64, QPAD), BF16),
        vmem((4, ROWS, QPAD), F32),
        vmem((2, TILES, TILE, 256), BF16),
        vmem((2, NT, TILE, 256), BF16),
        vmem((2, NT, TILE, 256), BF16),
        vmem((2, 2, QPAD, 256), BF16),
        vmem((NX, ROWS, QPAD), BF16),
        vmem((NX, ROWS, QPAD), BF16),
        vmem((2, NX, HALF, 512), F32),
        vmem((2, NX, HALF, 512), BF16),
        vmem((2, NX, HALF, 512), BF16),
        vmem((2, NX, HALF, 512), BF16),
        vmem((2, NX, HALF, 512), BF16),
        vmem((2, 4, HALF, 128), BF16),
        vmem((8, HALF, 128), BF16),
        vmem((HALF, 128), F32),
        vmem((HALF, 128), F32),
        dma((2,)),
        dma((2, TILES)), dma((2, NT)),
        dma((2, NT)), dma((2, TILES)),
        dma((2, 4, 2)), dma((2, 4, 2)), dma((2, 4, 2)), dma((2, 4, 2)),
        dma((NX,)), dma((NX,)),
        dma((2,)), dma((2,)),
        dma((2, NX)), dma((2, NX)),
        dma((2, 4)), dma((8,)),
        dma(()), dma(()),
    ]
    any_, in_vmem = pl.BlockSpec(memory_space=pl.ANY), pl.BlockSpec(memory_space=pltpu.VMEM)
    return pl.pallas_call(
        kernel,
        out_shape=jax.ShapeDtypeStruct((ROWS, 64), BF16),
        in_specs=[any_, in_vmem, any_, in_vmem],
        out_specs=in_vmem,
        scratch_shapes=scratch,
        compiler_params=pltpu.CompilerParams(
            collective_id=0, has_side_effects=True, vmem_limit_bytes=48 * 2**20
        ),
        name="rotated_projection",
    )(hidden_acts, mixing, packed_codes, exponents.reshape(8, 128))


def solution(mesh):
    placed = (P("dp", "tensor"), P(), P("tensor", None), P())
    return jax.shard_map(
        per_device, mesh=mesh, in_specs=placed, out_specs=P("dp", "tensor"), check_vma=False
    )
```

```python
import jax
import jax.numpy as jnp
from jax import lax
from jax.experimental import pallas as pl
from jax.experimental.pallas import tpu as pltpu
from jax.sharding import PartitionSpec as P

MESH = pl.DeviceIdType.MESH
NY, NX, NT = 8, 4, 16
ROWS = 256
HALF = ROWS // 2
INNER_M = 52
BLOCK = 3328
QUARTER = 832
QPAD = 896
SLICE = QPAD // NY
TILE = 16
TILES = SLICE // TILE
FIELDS = 4
COLS = 256
NEAR, FAR_UP, FAR_DOWN = (0, 112), (0, 64), (64, 48)
PARTS = ((0, 512), (512, 384))
F32, BF16 = jnp.float32, jnp.bfloat16


def iota(shape, dim):
    return lax.broadcasted_iota(jnp.int32, shape, dim)


def kernel(
    acts, mix, codes, expo, out,
    xbuf, cbuf, mixv, ebuf, mpad, gbuf, zbuf, s1, r1, s2, wbuf, ins, inr, pk, ces, cer, xs, xr, zs, zr, fs,
    lsem, s1s, s1r, s2s, s2r, us, ur, ds, dr, iss, irs, css, crs, xss, xrs, zss, zrs,
):
    dp = lax.axis_index("dp")
    t = lax.axis_index("tensor")
    y, x = dp // NX, dp % NX
    z, core = t // 2, t % 2
    sib = t + 1 - 2 * core
    up = ((y + 1) % NY) * NX + x
    down = ((y + NY - 1) % NY) * NX + x

    def along_t(dest):
        return (dp, dest)

    def along_x(dest):
        return (y * NX + dest, t)

    def rcopy(src, dst, ssem, rsem, dev):
        return pltpu.make_async_remote_copy(
            src_ref=src, dst_ref=dst, send_sem=ssem, recv_sem=rsem, device_id=dev, device_id_type=MESH
        )

    row0 = x * QUARTER + y * SLICE
    row1 = jnp.minimum(row0, BLOCK - SLICE)
    get_codes = pltpu.make_async_copy(
        codes.at[pl.ds(pl.multiple_of(row1, 16), SLICE)], cbuf.at[pl.ds(0, SLICE)], lsem.at[0]
    )
    get_acts = pltpu.make_async_copy(acts, xbuf, lsem.at[1])
    get_mix = pltpu.make_async_copy(mix, mixv, lsem.at[2])
    get_expo = pltpu.make_async_copy(expo, ebuf, lsem.at[3])
    get_codes.start()

    barrier = pltpu.get_barrier_semaphore()

    def greet(dev):
        pl.semaphore_signal(barrier, inc=1, device_id=dev, device_id_type=MESH)

    for o in range(1, NT):
        greet(along_t((t + o) % NT))
    for o in range(1, NX):
        greet(along_x((x + o) % NX))
    greet((up, t))
    greet((down, t))

    get_mix.start()
    get_acts.start()
    get_expo.start()
    cbuf[SLICE:, :] = jnp.zeros((64, COLS), jnp.int32)
    lane = iota((SLICE, 128), 1)
    get_codes.wait()
    words = cbuf[pl.ds(pl.multiple_of(row0 - row1, 16), SLICE), :]
    for k in range(FIELDS):
        field = jnp.right_shift(jnp.left_shift(words, 28 - 4 * k), 28).astype(F32)
        left, right = field[:, :128], field[:, 128:]
        for c, v in enumerate((
            jnp.where(lane < 64, left, pltpu.roll(right, 64, 1)),
            jnp.where(lane < 64, pltpu.roll(left, 64, 1), right),
        )):
            s1[k // 2, :, k % 2, :, 128 * c : 128 * c + 128] = v.astype(BF16).reshape(TILES, TILE, 128)
    pl.semaphore_wait(barrier, NT - 1 + NX - 1 + 2)

    def first(g, i):
        return rcopy(s1.at[g, i], r1.at[t], s1s.at[g, i], s1r.at[t], along_t(8 * g + i))

    for g in range(2):

        @pl.loop(0, TILES)
        def _(o):
            i = (t + o) % TILES

            @pl.when(8 * g + i != t)
            def _():
                first(g, i).start()

    mpad[...] = jnp.zeros_like(mpad)
    get_mix.wait()
    mpad[0:INNER_M, 0:INNER_M] = mixv[...]

    def block_of(v):
        return jnp.right_shift(v * 1261, 16)

    both = jnp.bitwise_and(iota((128, 128), 0), iota((128, 128), 1))
    both = jnp.bitwise_xor(both, jnp.right_shift(both, 2))
    both = jnp.bitwise_xor(both, jnp.right_shift(both, 1))
    had = (1 - 2 * jnp.bitwise_and(both, 1)).astype(F32).astype(BF16)
    cols = iota((128, QPAD), 1)
    inside = cols < QUARTER
    cblock = block_of(cols)
    which = iota((128, QPAD), 0)
    col_block = jnp.where(inside & (cblock == which), 1.0, 0.0).astype(BF16)
    col_inner = jnp.where(inside & (cols - INNER_M * cblock == which), 1.0, 0.0).astype(BF16)
    mixing = mpad[...].astype(BF16)
    right_m = jnp.dot(mixing, col_inner, preferred_element_type=F32).astype(BF16)
    right_h = jnp.dot(had, col_block, preferred_element_type=F32).astype(BF16)

    @pl.loop(0, 4)
    def _(blk):
        at = pl.multiple_of(blk * 240, 16)
        rows = iota((240, 128), 0) + (at - 64)
        ok = (rows >= 0) & (rows < QUARTER)
        rblock = block_of(rows)
        lane = iota((240, 128), 1)
        row_block = jnp.where(ok & (rblock == lane), 1.0, 0.0).astype(BF16)
        row_inner = jnp.where(ok & (rows - INNER_M * rblock == lane), 1.0, 0.0).astype(BF16)
        m_part = jnp.dot(row_inner, right_m, preferred_element_type=F32)
        h_part = jnp.dot(row_block, right_h, preferred_element_type=F32)
        gbuf[pl.ds(at, 240)] = (m_part * h_part).astype(BF16)

    get_acts.wait()

    def spread(q, part):
        lo, n = PARTS[part]
        cut = pl.ds(lo, n)
        return rcopy(
            ins.at[q, :, cut], inr.at[x, :, cut], iss.at[q, part], irs.at[x, part], along_x(q)
        )

    for part, (lo, n) in enumerate(PARTS):
        for q in range(4):
            at = q * QUARTER - 64 * (q % 2)
            g = gbuf[0:QPAD, lo : lo + n] if q % 2 else gbuf[64 : 64 + QPAD, lo : lo + n]
            zbuf[q, :, 0:n] = jnp.dot(xbuf[:, at : at + QPAD], g, preferred_element_type=F32)

        @pl.loop(0, ROWS // 16)
        def _(blk):
            rows = pl.ds(pl.multiple_of(blk * 16, 16), 16)
            z0, z1, z2, z3 = (zbuf[q, rows, 0:n] for q in range(4))
            u0, u1, u2, u3 = z0 + z1, z0 - z1, z2 + z3, z2 - z3
            for q, v in enumerate((u0 + u2, u1 + u3, u0 - u2, u1 - u3)):
                ins[q, rows, lo : lo + n] = (v * 0.125).astype(BF16)

        for d in (2, 1, 3):
            spread((x + d) % NX, part).start()

    g0, i0 = t // 8, t % 8

    def tile_at(g, i):
        return wbuf.at[pl.ds(2 * g, 2), pl.ds(pl.multiple_of(y * SLICE + i * TILE, 16), TILE)]

    def second(a):
        return rcopy(s2.at[a], tile_at(g0, i0), s2s.at[a], s2r.at[g0, i0], along_t(a))

    @pl.when(i0 < TILES)
    def _():
        @pl.loop(1, NT)
        def _(o):
            b = (t + o) % NT
            rcopy(s1.at[0, 0], r1.at[b], s1s.at[0, 0], s1r.at[b], along_t(b)).wait_recv()

        r1[t] = s1[g0, i0]
        for f in range(2):
            for half in range(2):
                lanes = slice(128 * half, 128 * half + 128)
                v = [r1[b, f, :, lanes].astype(F32) for b in range(NT)]
                for bit in (1, 2, 4, 8):
                    v = [v[a ^ bit] - v[a] if a & bit else v[a] + v[a ^ bit] for a in range(NT)]
                for a in range(NT):
                    s2[a, f, :, lanes] = v[a].astype(BF16)

        @pl.loop(1, NT)
        def _(o):
            second((t + o) % NT).start()

        for f in range(2):
            wbuf[2 * g0 + f, pl.ds(pl.multiple_of(y * SLICE + i0 * TILE, 16), TILE), :] = s2[t, f]

    inr[x] = ins[x]

    def assembled(g):
        @pl.loop(0, TILES)
        def _(i):
            @pl.when(8 * g + i != t)
            def _():
                rcopy(s2.at[0], tile_at(g, i), s2s.at[0], s2r.at[g, i], along_t(8 * g + i)).wait_recv()

    def hop(k, step, sign, away):
        yy = (y - sign * away + NY) % NY
        off, n = NEAR if step < 3 else FAR_UP if sign > 0 else FAR_DOWN
        part = wbuf.at[k, pl.ds(pl.multiple_of(yy * SLICE + off, 16), n)]
        if sign > 0:
            return rcopy(part, part, us.at[k, step], ur.at[k, step], (up, t))
        return rcopy(part, part, ds.at[k, step], dr.at[k, step], (down, t))

    def ring(k, s):
        for sign in (1, -1):
            if s:
                hop(k, s - 1, sign, s).wait_recv()
            if s < 4:
                hop(k, s, sign, s).start()

    def swap_cores(k):
        return rcopy(ces.at[k], cer.at[k], css.at[k], crs.at[k], along_t(sib))

    def partials(k):
        w = wbuf[k]
        for p in range(NX):
            v = jnp.dot(inr[p], w, preferred_element_type=F32)
            ces[k, p] = jnp.where(core == 0, v[:, 128:], v[:, :128]).astype(BF16)
            pk[k, p] = jnp.where(core == 0, v[:, :128], v[:, 128:])
        swap_cores(k).start()

    def over_x(k, p):
        return rcopy(xs.at[k, p], xr.at[k, x], xss.at[k, p], xrs.at[k, x], along_x(p))

    def reduce_x(k):
        swap_cores(k).wait_recv()
        for p in range(NX):
            v = pk[k, p] + cer[k, p].astype(F32)
            pk[k, p] = v
            xs[k, p] = v.astype(BF16)
        for d in (2, 1, 3):
            over_x(k, (x + d) % NX).start()

    def over_z(k, i):
        return rcopy(zs.at[k, i], zr.at[z], zss.at[k, i], zrs.at[z], along_t(2 * (2 * k + i) + core))

    lane1 = iota((HALF, 128), 1)

    def reduce_z(k):
        for d in (1, 3, 2):
            src = (x + d) % NX
            rcopy(xs.at[k, 0], xr.at[k, src], xss.at[k, 0], xrs.at[k, src], along_x(src)).wait_recv()
        total = pk[k, x]
        for d in (1, 2, 3):
            total = total + xr[k, (x + d) % NX].astype(F32)
        top, low = total[:HALF], total[HALF:]
        packed = (
            jnp.where(lane1 < 64, top, pltpu.roll(low, 64, 1)),
            jnp.where(lane1 < 64, pltpu.roll(top, 64, 1), low),
        )
        for i in range(2):
            zs[k, i] = packed[i].astype(BF16)

            @pl.when(2 * k + i != z)
            def _():
                over_z(k, i).start()

            @pl.when(2 * k + i == z)
            def _():
                fs[...] = packed[i]

    assembled(0)
    ring(0, 0)
    ring(1, 0)
    assembled(1)
    ring(2, 0)
    ring(0, 1)
    ring(3, 0)
    ring(1, 1)
    ring(2, 1)
    ring(0, 2)
    ring(3, 1)
    ring(1, 2)
    ring(2, 2)
    ring(0, 3)
    ring(3, 2)
    ring(1, 3)
    ring(2, 3)
    for d in (1, 3, 2):
        src = (x + d) % NX
        for part, (lo, n) in enumerate(PARTS):
            cut = pl.ds(lo, n)
            rcopy(
                ins.at[0, :, cut], inr.at[src, :, cut], iss.at[0, part], irs.at[src, part], along_x(src)
            ).wait_recv()
    ring(0, 4)
    partials(0)
    ring(3, 3)
    ring(1, 4)
    reduce_x(0)
    partials(1)
    ring(2, 4)
    reduce_x(1)
    partials(2)
    ring(3, 4)
    reduce_x(2)
    partials(3)
    reduce_z(0)
    reduce_x(3)

    for g in range(2):

        @pl.loop(0, TILES)
        def _(i):
            @pl.when(8 * g + i != t)
            def _():
                first(g, i).wait_send()

    @pl.when(i0 < TILES)
    def _():
        @pl.loop(1, NT)
        def _(o):
            second((t + o) % NT).wait_send()

    for d in (1, 2, 3):
        for part in range(2):
            spread((x + d) % NX, part).wait_send()
    for k in range(FIELDS):
        for s in range(4):
            hop(k, s, 1, s).wait_send()
            hop(k, s, -1, s).wait_send()
        swap_cores(k).wait_send()

    reduce_z(1)
    reduce_z(2)
    reduce_z(3)
    for k in range(FIELDS):
        for d in (1, 2, 3):
            over_x(k, (x + d) % NX).wait_send()

    get_expo.wait()
    lane8 = iota((8, 128), 1)
    e = ebuf[...]
    mpad[0:8, :] = jnp.where(
        (lane8 < 64) == (core == 0), jnp.left_shift(1, e + 16), jnp.left_shift(1, pltpu.roll(e, 64, 1) + 16)
    ).astype(F32)

    def total_of_z(o, acc):
        src = (z + o) % 8
        rcopy(zs.at[0, 0], zr.at[src], zss.at[0, 0], zrs.at[src], along_t(2 * src + core)).wait_recv()
        return acc + zr[src].astype(F32)

    total = lax.fori_loop(1, 8, total_of_z, fs[...])
    total = total * (mpad[pl.ds(z, 1), :] * (2.0 ** -28))
    out[0:HALF, :] = total[:, :64].astype(BF16)
    out[HALF:ROWS, :] = pltpu.roll(total, 64, 1)[:, :64].astype(BF16)
    for k in range(FIELDS):
        for i in range(2):

            @pl.when(2 * k + i != z)
            def _():
                over_z(k, i).wait_send()


def per_device(hidden_acts, mixing, packed_codes, exponents):
    vmem = pltpu.VMEM
    dma = pltpu.SemaphoreType.DMA
    scratch = [
        vmem((ROWS, BLOCK), BF16),
        vmem((SLICE + 64, COLS), jnp.int32),
        vmem((INNER_M, INNER_M), F32),
        vmem((8, 128), jnp.int32),
        vmem((128, 128), F32),
        vmem((QPAD + 64, QPAD), BF16),
        vmem((4, ROWS, 512), F32),
        vmem((2, TILES, 2, TILE, COLS), BF16),
        vmem((NT, 2, TILE, COLS), BF16),
        vmem((NT, 2, TILE, COLS), BF16),
        vmem((FIELDS, QPAD, COLS), BF16),
        vmem((NX, ROWS, QPAD), BF16),
        vmem((NX, ROWS, QPAD), BF16),
        vmem((FIELDS, NX, ROWS, 128), F32),
        vmem((FIELDS, NX, ROWS, 128), BF16),
        vmem((FIELDS, NX, ROWS, 128), BF16),
        vmem((FIELDS, NX, ROWS, 128), BF16),
        vmem((FIELDS, NX, ROWS, 128), BF16),
        vmem((FIELDS, 2, HALF, 128), BF16),
        vmem((8, HALF, 128), BF16),
        vmem((HALF, 128), F32),
        dma((4,)),
        dma((2, TILES)), dma((NT,)),
        dma((NT,)), dma((2, TILES)),
        dma((FIELDS, 4)), dma((FIELDS, 4)), dma((FIELDS, 4)), dma((FIELDS, 4)),
        dma((NX, 2)), dma((NX, 2)),
        dma((FIELDS,)), dma((FIELDS,)),
        dma((FIELDS, NX)), dma((FIELDS, NX)),
        dma((FIELDS, 2)), dma((8,)),
    ]
    in_hbm, in_vmem = pl.BlockSpec(memory_space=pltpu.HBM), pl.BlockSpec(memory_space=pltpu.VMEM)
    return pl.pallas_call(
        kernel,
        out_shape=jax.ShapeDtypeStruct((ROWS, 64), BF16),
        in_specs=[in_hbm] * 4,
        out_specs=in_vmem,
        scratch_shapes=scratch,
        compiler_params=pltpu.CompilerParams(
            collective_id=0, has_side_effects=True, vmem_limit_bytes=62 * 2**20
        ),
        name="rotated_projection",
    )(hidden_acts, mixing, packed_codes, exponents.reshape(8, 128))


def solution(mesh):
    placed = (P("dp", "tensor"), P(), P("tensor", None), P())
    return jax.shard_map(
        per_device, mesh=mesh, in_specs=placed, out_specs=P("dp", "tensor"), check_vma=False
    )
```

```python
import jax
import jax.numpy as jnp
from jax import lax
from jax.experimental import pallas as pl
from jax.experimental.pallas import tpu as pltpu
from jax.sharding import PartitionSpec as P

MESH = pl.DeviceIdType.MESH
NY, NX, NT = 8, 4, 16
ROWS = 256
HALF = ROWS // 2
INNER_M = 52
BLOCK = 3328
QUARTER = 832
QPAD = 896
SLICE = QPAD // NY
TILE = 16
TILES = SLICE // TILE
CHUNKS = 4
COLS = 256
NEAR, FAR_UP, FAR_DOWN = (0, 112), (0, 64), (64, 48)
PARTS = ((0, 512), (512, 384))
F32, BF16 = jnp.float32, jnp.bfloat16


def iota(shape, dim):
    return lax.broadcasted_iota(jnp.int32, shape, dim)


def kernel(
    acts, mix, codes, expo, out,
    xbuf, cbuf, mixv, ebuf, mpad, gbuf, zbuf, s1, r1, s2, wbuf, ins, inr, pk, ces, cer, xs, xr, zs, zr, fs,
    lsem, s1s, s1r, s2s, s2r, us, ur, ds, dr, iss, irs, css, crs, xss, xrs, zss, zrs,
):
    dp = lax.axis_index("dp")
    t = lax.axis_index("tensor")
    y, x = dp // NX, dp % NX
    z, core = t // 2, t % 2
    sib = t + 1 - 2 * core
    up = ((y + 1) % NY) * NX + x
    down = ((y + NY - 1) % NY) * NX + x

    def along_t(dest):
        return (dp, dest)

    def along_x(dest):
        return (y * NX + dest, t)

    def rcopy(src, dst, ssem, rsem, dev):
        return pltpu.make_async_remote_copy(
            src_ref=src, dst_ref=dst, send_sem=ssem, recv_sem=rsem, device_id=dev, device_id_type=MESH
        )

    row0 = x * QUARTER + y * SLICE
    row1 = jnp.minimum(row0, BLOCK - SLICE)
    get_codes = pltpu.make_async_copy(
        codes.at[pl.ds(pl.multiple_of(row1, 16), SLICE)], cbuf.at[pl.ds(0, SLICE)], lsem.at[0]
    )
    get_acts = pltpu.make_async_copy(acts, xbuf, lsem.at[1])
    get_mix = pltpu.make_async_copy(mix, mixv, lsem.at[2])
    get_expo = pltpu.make_async_copy(expo, ebuf, lsem.at[3])
    get_codes.start()

    barrier = pltpu.get_barrier_semaphore()

    def greet(dev):
        pl.semaphore_signal(barrier, inc=1, device_id=dev, device_id_type=MESH)

    for o in range(1, NT):
        greet(along_t((t + o) % NT))
    for o in range(1, NX):
        greet(along_x((x + o) % NX))
    greet((up, t))
    greet((down, t))

    get_mix.start()
    get_acts.start()
    get_expo.start()
    cbuf[SLICE:, :] = jnp.zeros((64, COLS), jnp.int32)
    lane = iota((SLICE, 128), 1)
    get_codes.wait()
    words = cbuf[pl.ds(pl.multiple_of(row0 - row1, 16), SLICE), :]
    fields = [jnp.right_shift(jnp.left_shift(words, 28 - 4 * f), 28).astype(F32) for f in range(4)]
    for k in range(CHUNKS):
        half = slice(128 * (k % 2), 128 * (k % 2) + 128)
        left, right = fields[k // 2][:, half], fields[k // 2 + 2][:, half]
        s1[k, :, :, 0:128] = (
            jnp.where(lane < 64, left, pltpu.roll(right, 64, 1)).astype(BF16).reshape(TILES, TILE, 128)
        )
        s1[k, :, :, 128:256] = (
            jnp.where(lane < 64, pltpu.roll(left, 64, 1), right).astype(BF16).reshape(TILES, TILE, 128)
        )
    pl.semaphore_wait(barrier, NT - 1 + NX - 1 + 2)

    def owner(k, i):
        return (TILES * k + i) % NT

    def first(k, i):
        return rcopy(s1.at[k, i], r1.at[k, t], s1s.at[k, i], s1r.at[k, t], along_t(owner(k, i)))

    for k in range(CHUNKS):

        @pl.loop(0, TILES)
        def _(o):
            i = (t + o) % TILES

            @pl.when(owner(k, i) != t)
            def _():
                first(k, i).start()

    mpad[...] = jnp.zeros_like(mpad)
    get_mix.wait()
    mpad[0:INNER_M, 0:INNER_M] = mixv[...]

    def block_of(v):
        return jnp.right_shift(v * 1261, 16)

    both = jnp.bitwise_and(iota((128, 128), 0), iota((128, 128), 1))
    both = jnp.bitwise_xor(both, jnp.right_shift(both, 2))
    both = jnp.bitwise_xor(both, jnp.right_shift(both, 1))
    had = (1 - 2 * jnp.bitwise_and(both, 1)).astype(F32).astype(BF16)
    cols = iota((128, QPAD), 1)
    inside = cols < QUARTER
    cblock = block_of(cols)
    which = iota((128, QPAD), 0)
    col_block = jnp.where(inside & (cblock == which), 1.0, 0.0).astype(BF16)
    col_inner = jnp.where(inside & (cols - INNER_M * cblock == which), 1.0, 0.0).astype(BF16)
    mixing = mpad[...].astype(BF16)
    right_m = jnp.dot(mixing, col_inner, preferred_element_type=F32).astype(BF16)
    right_h = jnp.dot(had, col_block, preferred_element_type=F32).astype(BF16)

    @pl.loop(0, 4)
    def _(blk):
        at = pl.multiple_of(blk * 240, 16)
        rows = iota((240, 128), 0) + (at - 64)
        ok = (rows >= 0) & (rows < QUARTER)
        rblock = block_of(rows)
        lane = iota((240, 128), 1)
        row_block = jnp.where(ok & (rblock == lane), 1.0, 0.0).astype(BF16)
        row_inner = jnp.where(ok & (rows - INNER_M * rblock == lane), 1.0, 0.0).astype(BF16)
        m_part = jnp.dot(row_inner, right_m, preferred_element_type=F32)
        h_part = jnp.dot(row_block, right_h, preferred_element_type=F32)
        gbuf[pl.ds(at, 240)] = (m_part * h_part).astype(BF16)

    get_acts.wait()

    def spread(q, part):
        lo, n = PARTS[part]
        cut = pl.ds(lo, n)
        return rcopy(
            ins.at[q, :, cut], inr.at[x, :, cut], iss.at[q, part], irs.at[x, part], along_x(q)
        )

    for part, (lo, n) in enumerate(PARTS):
        for q in range(4):
            at = q * QUARTER - 64 * (q % 2)
            g = gbuf[0:QPAD, lo : lo + n] if q % 2 else gbuf[64 : 64 + QPAD, lo : lo + n]
            zbuf[q, :, 0:n] = jnp.dot(xbuf[:, at : at + QPAD], g, preferred_element_type=F32)

        @pl.loop(0, ROWS // 16)
        def _(blk):
            rows = pl.ds(pl.multiple_of(blk * 16, 16), 16)
            z0, z1, z2, z3 = (zbuf[q, rows, 0:n] for q in range(4))
            u0, u1, u2, u3 = z0 + z1, z0 - z1, z2 + z3, z2 - z3
            for q, v in enumerate((u0 + u2, u1 + u3, u0 - u2, u1 - u3)):
                ins[q, rows, lo : lo + n] = (v * 0.125).astype(BF16)

        for d in (2, 1, 3):
            spread((x + d) % NX, part).start()

    def tile_at(k, i):
        return wbuf.at[k, pl.ds(pl.multiple_of(y * SLICE + i * TILE, 16), TILE)]

    def mine(k):
        return (t + 4 * NT - TILES * k) % NT

    def second(k, a):
        i = mine(k)
        return rcopy(s2.at[k, a], tile_at(k, i), s2s.at[k, a], s2r.at[k, i], along_t(a))

    for k in range(CHUNKS):

        @pl.when(mine(k) < TILES)
        def _():
            @pl.loop(1, NT)
            def _(o):
                b = (t + o) % NT
                rcopy(s1.at[k, 0], r1.at[k, b], s1s.at[k, 0], s1r.at[k, b], along_t(b)).wait_recv()

            i = mine(k)
            r1[k, t] = s1[k, i]
            for half in range(2):
                lanes = slice(128 * half, 128 * half + 128)
                v = [r1[k, b, :, lanes].astype(F32) for b in range(NT)]
                for bit in (1, 2, 4, 8):
                    v = [v[a ^ bit] - v[a] if a & bit else v[a] + v[a ^ bit] for a in range(NT)]
                for a in range(NT):
                    s2[k, a, :, lanes] = v[a].astype(BF16)

            @pl.loop(1, NT)
            def _(o):
                second(k, (t + o) % NT).start()

            wbuf[k, pl.ds(pl.multiple_of(y * SLICE + i * TILE, 16), TILE), :] = s2[k, t]

    inr[x] = ins[x]

    def assembled(k):
        @pl.loop(0, TILES)
        def _(i):
            @pl.when(owner(k, i) != t)
            def _():
                rcopy(s2.at[k, 0], tile_at(k, i), s2s.at[k, 0], s2r.at[k, i], along_t(owner(k, i))).wait_recv()

    def hop(k, step, sign, away):
        yy = (y - sign * away + NY) % NY
        off, n = NEAR if step < 3 else FAR_UP if sign > 0 else FAR_DOWN
        part = wbuf.at[k, pl.ds(pl.multiple_of(yy * SLICE + off, 16), n)]
        if sign > 0:
            return rcopy(part, part, us.at[k, step], ur.at[k, step], (up, t))
        return rcopy(part, part, ds.at[k, step], dr.at[k, step], (down, t))

    def ring(k, s):
        for sign in (1, -1):
            if s:
                hop(k, s - 1, sign, s).wait_recv()
            if s < 4:
                hop(k, s, sign, s).start()

    def swap_cores(k):
        return rcopy(ces.at[k], cer.at[k], css.at[k], crs.at[k], along_t(sib))

    def partials(k):
        w = wbuf[k]
        for p in range(NX):
            v = jnp.dot(inr[p], w, preferred_element_type=F32)
            ces[k, p] = jnp.where(core == 0, v[:, 128:], v[:, :128]).astype(BF16)
            pk[k, p] = jnp.where(core == 0, v[:, :128], v[:, 128:])
        swap_cores(k).start()

    def over_x(k, p):
        return rcopy(xs.at[k, p], xr.at[k, x], xss.at[k, p], xrs.at[k, x], along_x(p))

    def reduce_x(k):
        swap_cores(k).wait_recv()
        for p in range(NX):
            v = pk[k, p] + cer[k, p].astype(F32)
            pk[k, p] = v
            xs[k, p] = v.astype(BF16)
        for d in (2, 1, 3):
            over_x(k, (x + d) % NX).start()

    def over_z(k, i):
        return rcopy(zs.at[k, i], zr.at[z], zss.at[k, i], zrs.at[z], along_t(2 * (k + 4 * i) + core))

    lane1 = iota((HALF, 128), 1)

    def reduce_z(k):
        for d in (1, 3, 2):
            src = (x + d) % NX
            rcopy(xs.at[k, 0], xr.at[k, src], xss.at[k, 0], xrs.at[k, src], along_x(src)).wait_recv()
        total = pk[k, x]
        for d in (1, 2, 3):
            total = total + xr[k, (x + d) % NX].astype(F32)
        top, low = total[:HALF], total[HALF:]
        packed = (
            jnp.where(lane1 < 64, top, pltpu.roll(low, 64, 1)),
            jnp.where(lane1 < 64, pltpu.roll(top, 64, 1), low),
        )
        for i in range(2):
            zs[k, i] = packed[i].astype(BF16)

            @pl.when(k + 4 * i != z)
            def _():
                over_z(k, i).start()

            @pl.when(k + 4 * i == z)
            def _():
                fs[...] = packed[i]

    assembled(0)
    ring(0, 0)
    assembled(1)
    ring(1, 0)
    assembled(2)
    ring(2, 0)
    ring(0, 1)
    ring(1, 1)
    assembled(3)
    ring(3, 0)
    ring(0, 2)
    ring(2, 1)
    ring(1, 2)
    ring(0, 3)
    ring(3, 1)
    ring(2, 2)
    ring(1, 3)
    for d in (1, 3, 2):
        src = (x + d) % NX
        for part, (lo, n) in enumerate(PARTS):
            cut = pl.ds(lo, n)
            rcopy(
                ins.at[0, :, cut], inr.at[src, :, cut], iss.at[0, part], irs.at[src, part], along_x(src)
            ).wait_recv()
    ring(0, 4)
    partials(0)
    ring(3, 2)
    reduce_x(0)
    ring(2, 3)
    ring(1, 4)
    partials(1)
    ring(3, 3)
    reduce_x(1)
    ring(2, 4)
    partials(2)
    reduce_x(2)
    ring(3, 4)
    partials(3)
    reduce_z(0)
    reduce_x(3)

    for k in range(CHUNKS):

        @pl.loop(0, TILES)
        def _(i):
            @pl.when(owner(k, i) != t)
            def _():
                first(k, i).wait_send()

        @pl.when(mine(k) < TILES)
        def _():
            @pl.loop(1, NT)
            def _(o):
                second(k, (t + o) % NT).wait_send()

    for d in (1, 2, 3):
        for part in range(2):
            spread((x + d) % NX, part).wait_send()
    for k in range(CHUNKS):
        for s in range(4):
            hop(k, s, 1, s).wait_send()
            hop(k, s, -1, s).wait_send()
        swap_cores(k).wait_send()

    reduce_z(1)
    reduce_z(2)
    reduce_z(3)
    for k in range(CHUNKS):
        for d in (1, 2, 3):
            over_x(k, (x + d) % NX).wait_send()

    get_expo.wait()
    lane8 = iota((8, 128), 1)
    e = ebuf[...]
    mpad[0:8, :] = jnp.where(
        (lane8 < 64) == (core == 0), jnp.left_shift(1, e + 16), jnp.left_shift(1, pltpu.roll(e, 64, 1) + 16)
    ).astype(F32)

    def total_of_z(o, acc):
        src = (z + o) % 8
        rcopy(zs.at[0, 0], zr.at[src], zss.at[0, 0], zrs.at[src], along_t(2 * src + core)).wait_recv()
        return acc + zr[src].astype(F32)

    total = lax.fori_loop(1, 8, total_of_z, fs[...])
    total = total * (mpad[pl.ds(z, 1), :] * (2.0 ** -28))
    turned = total.T
    out[:, 0:HALF] = turned[0:64].astype(BF16)
    out[:, HALF:ROWS] = turned[64:128].astype(BF16)
    for k in range(CHUNKS):
        for i in range(2):

            @pl.when(k + 4 * i != z)
            def _():
                over_z(k, i).wait_send()


def per_device(hidden_acts, mixing, packed_codes, exponents):
    vmem = pltpu.VMEM
    dma = pltpu.SemaphoreType.DMA
    scratch = [
        vmem((ROWS, BLOCK), BF16),
        vmem((SLICE + 64, COLS), jnp.int32),
        vmem((INNER_M, INNER_M), F32),
        vmem((8, 128), jnp.int32),
        vmem((128, 128), F32),
        vmem((QPAD + 64, QPAD), BF16),
        vmem((4, ROWS, 512), F32),
        vmem((CHUNKS, TILES, TILE, COLS), BF16),
        vmem((CHUNKS, NT, TILE, COLS), BF16),
        vmem((CHUNKS, NT, TILE, COLS), BF16),
        vmem((CHUNKS, QPAD, COLS), BF16),
        vmem((NX, ROWS, QPAD), BF16),
        vmem((NX, ROWS, QPAD), BF16),
        vmem((CHUNKS, NX, ROWS, 128), F32),
        vmem((CHUNKS, NX, ROWS, 128), BF16),
        vmem((CHUNKS, NX, ROWS, 128), BF16),
        vmem((CHUNKS, NX, ROWS, 128), BF16),
        vmem((CHUNKS, NX, ROWS, 128), BF16),
        vmem((CHUNKS, 2, HALF, 128), BF16),
        vmem((8, HALF, 128), BF16),
        vmem((HALF, 128), F32),
        dma((4,)),
        dma((CHUNKS, TILES)), dma((CHUNKS, NT)),
        dma((CHUNKS, NT)), dma((CHUNKS, TILES)),
        dma((CHUNKS, 4)), dma((CHUNKS, 4)), dma((CHUNKS, 4)), dma((CHUNKS, 4)),
        dma((NX, 2)), dma((NX, 2)),
        dma((CHUNKS,)), dma((CHUNKS,)),
        dma((CHUNKS, NX)), dma((CHUNKS, NX)),
        dma((CHUNKS, 2)), dma((8,)),
    ]
    in_hbm, in_vmem = pl.BlockSpec(memory_space=pltpu.HBM), pl.BlockSpec(memory_space=pltpu.VMEM)
    return pl.pallas_call(
        kernel,
        out_shape=jax.ShapeDtypeStruct((64, ROWS), BF16),
        in_specs=[in_hbm] * 4,
        out_specs=in_vmem,
        scratch_shapes=scratch,
        compiler_params=pltpu.CompilerParams(
            collective_id=0, has_side_effects=True, vmem_limit_bytes=62 * 2**20
        ),
        name="rotated_projection",
    )(hidden_acts, mixing, packed_codes, exponents.reshape(8, 128)).T


def solution(mesh):
    placed = (P("dp", "tensor"), P(), P("tensor", None), P())
    return jax.shard_map(
        per_device, mesh=mesh, in_specs=placed, out_specs=P("dp", "tensor"), check_vma=False
    )
```

```python
import jax
import jax.numpy as jnp
from jax import lax
from jax.experimental import pallas as pl
from jax.experimental.pallas import tpu as pltpu
from jax.sharding import PartitionSpec as P

MESH = pl.DeviceIdType.MESH
NY, NX, NT = 8, 4, 16
ROWS = 256
HALF = ROWS // 2
INNER_M = 52
BLOCK = 3328
QUARTER = 832
QPAD = 896
TAKEN = 640
REST = QUARTER - TAKEN
DIRECT = 4 * REST
SLICE = TAKEN // NY
TILE = 16
TILES = SLICE // TILE
CHUNKS = 4
COLS = 256
FAR = 48, 32
F32, BF16 = jnp.float32, jnp.bfloat16


def iota(shape, dim):
    return lax.broadcasted_iota(jnp.int32, shape, dim)


def kernel(
    acts, mix, codes, expo, out,
    xbuf, cbuf, dbuf, mixv, ebuf, mpad, gbuf, zbuf, s1, r1, s2, wbuf, ins, inr, pk, ces, cer, xs, xr, zs, zr, fs,
    own, acs, a1, a2, a3, pa, aces, acer,
    lsem, s1s, s1r, s2s, s2r, us, ur, ds, dr, iss, irs, css, crs, xss, xrs, zss, zrs, a1s, a1r, a3s, a3r, asem,
):
    dp = lax.axis_index("dp")
    t = lax.axis_index("tensor")
    y, x = dp // NX, dp % NX
    z, core = t // 2, t % 2
    sib = t + 1 - 2 * core
    up = ((y + 1) % NY) * NX + x
    down = ((y + NY - 1) % NY) * NX + x

    def along_t(dest):
        return (dp, dest)

    def along_x(dest):
        return (y * NX + dest, t)

    def rcopy(src, dst, ssem, rsem, dev):
        return pltpu.make_async_remote_copy(
            src_ref=src, dst_ref=dst, send_sem=ssem, recv_sem=rsem, device_id=dev, device_id_type=MESH
        )

    row0 = pl.multiple_of(x * QUARTER + y * SLICE, 16)
    get_codes = pltpu.make_async_copy(codes.at[pl.ds(row0, SLICE)], cbuf, lsem.at[0])
    get_acts = pltpu.make_async_copy(acts, xbuf, lsem.at[1])
    get_mix = pltpu.make_async_copy(mix, mixv, lsem.at[2])
    get_expo = pltpu.make_async_copy(expo, ebuf, lsem.at[3])
    get_own = []
    for u in range(2):
        for at, row, n in (
            (0, 2 * u * QUARTER + TAKEN, 192),
            (192, (2 * u + 1) * QUARTER + TAKEN + 128, 64),
            (256, (2 * u + 1) * QUARTER + TAKEN, 128),
        ):
            get_own.append(pltpu.make_async_copy(
                codes.at[pl.ds(row, n)], dbuf.at[pl.ds(384 * u + at, n)], lsem.at[4 + len(get_own)]
            ))
    get_codes.start()

    barrier = pltpu.get_barrier_semaphore()

    def greet(dev):
        pl.semaphore_signal(barrier, inc=1, device_id=dev, device_id_type=MESH)

    for o in range(1, NT):
        greet(along_t((t + o) % NT))
    for o in range(1, NX):
        greet(along_x((x + o) % NX))
    greet((up, t))
    greet((down, t))

    get_mix.start()
    get_acts.start()
    get_expo.start()
    for g in get_own:
        g.start()
    get_codes.wait()

    def unpacked(words):
        lane = iota((words.shape[0], 128), 1)
        fields = [jnp.right_shift(jnp.left_shift(words, 28 - 4 * f), 28).astype(F32) for f in range(4)]
        for k in range(CHUNKS):
            half = slice(128 * (k % 2), 128 * (k % 2) + 128)
            left, right = fields[k // 2][:, half], fields[k // 2 + 2][:, half]
            yield (
                jnp.where(lane < 64, left, pltpu.roll(right, 64, 1)).astype(BF16),
                jnp.where(lane < 64, pltpu.roll(left, 64, 1), right).astype(BF16),
            )

    for k, halves in enumerate(unpacked(cbuf[...])):
        for c in range(2):
            s1[k, :, :, 128 * c : 128 * c + 128] = halves[c].reshape(TILES, TILE, 128)
    mpad[...] = jnp.zeros_like(mpad)
    get_mix.wait()
    mpad[0:INNER_M, 0:INNER_M] = mixv[...]

    def block_of(v):
        return jnp.right_shift(v * 1261, 16)

    both = jnp.bitwise_and(iota((128, 128), 0), iota((128, 128), 1))
    both = jnp.bitwise_xor(both, jnp.right_shift(both, 2))
    both = jnp.bitwise_xor(both, jnp.right_shift(both, 1))
    had = (1 - 2 * jnp.bitwise_and(both, 1)).astype(F32).astype(BF16)
    cols = iota((128, QPAD), 1)
    inside = cols < QUARTER
    cblock = block_of(cols)
    which = iota((128, QPAD), 0)
    col_block = jnp.where(inside & (cblock == which), 1.0, 0.0).astype(BF16)
    col_inner = jnp.where(inside & (cols - INNER_M * cblock == which), 1.0, 0.0).astype(BF16)
    mixing = mpad[...].astype(BF16)
    right_m = jnp.dot(mixing, col_inner, preferred_element_type=F32).astype(BF16)
    right_h = jnp.dot(had, col_block, preferred_element_type=F32).astype(BF16)

    @pl.loop(0, 4)
    def _(blk):
        at = pl.multiple_of(blk * 240, 16)
        rows = iota((240, 128), 0) + (at - 64)
        ok = (rows >= 0) & (rows < QUARTER)
        rblock = block_of(rows)
        lane = iota((240, 128), 1)
        row_block = jnp.where(ok & (rblock == lane), 1.0, 0.0).astype(BF16)
        row_inner = jnp.where(ok & (rows - INNER_M * rblock == lane), 1.0, 0.0).astype(BF16)
        m_part = jnp.dot(row_inner, right_m, preferred_element_type=F32)
        h_part = jnp.dot(row_block, right_h, preferred_element_type=F32)
        gbuf[pl.ds(at, 240)] = (m_part * h_part).astype(BF16)

    pl.semaphore_wait(barrier, NT - 1 + NX - 1 + 2)

    def owner(k, i):
        return (TILES * k + i) % NT

    def first(k, i):
        return rcopy(s1.at[k, i], r1.at[k, t], s1s.at[k, i], s1r.at[k, t], along_t(owner(k, i)))

    for k in range(CHUNKS):

        @pl.loop(0, TILES)
        def _(o):
            i = (t + o) % TILES

            @pl.when(owner(k, i) != t)
            def _():
                first(k, i).start()

    get_acts.wait()

    def spread(q):
        return rcopy(ins.at[q], inr.at[x], iss.at[q], irs.at[x], along_x(q))

    def inner(lo, n, put):
        for q in range(4):
            at = q * QUARTER - 64 * (q % 2)
            g = gbuf[0:QPAD, lo : lo + n] if q % 2 else gbuf[64 : 64 + QPAD, lo : lo + n]
            zbuf[q, :, 0:n] = jnp.dot(xbuf[:, at : at + QPAD], g, preferred_element_type=F32)

        @pl.loop(0, ROWS // 16)
        def _(blk):
            rows = pl.ds(pl.multiple_of(blk * 16, 16), 16)
            z0, z1, z2, z3 = (zbuf[q, rows, 0:n] for q in range(4))
            u0, u1, u2, u3 = z0 + z1, z0 - z1, z2 + z3, z2 - z3
            put(blk, rows, [v * 0.125 for v in (u0 + u2, u1 + u3, u0 - u2, u1 - u3)])

    def put_taken(blk, rows, quarters):
        for q, v in enumerate(quarters):
            ins[q, rows, :] = v.astype(BF16)

    inner(0, TAKEN, put_taken)
    for d in (2, 1, 3):
        spread((x + d) % NX).start()

    def tile_at(k, i):
        return wbuf.at[k, pl.ds(pl.multiple_of(y * SLICE + i * TILE, 16), TILE)]

    def mine(k):
        return (t + 4 * NT - TILES * k) % NT

    def second(k, a):
        i = mine(k)
        return rcopy(s2.at[k, a], tile_at(k, i), s2s.at[k, a], s2r.at[k, i], along_t(a))

    def butterfly(v):
        for bit in (1, 2, 4, 8):
            v = [v[a ^ bit] - v[a] if a & bit else v[a] + v[a ^ bit] for a in range(NT)]
        return v

    for k in range(CHUNKS):

        @pl.when(mine(k) < TILES)
        def _():
            @pl.loop(1, NT)
            def _(o):
                b = (t + o) % NT
                rcopy(s1.at[k, 0], r1.at[k, b], s1s.at[k, 0], s1r.at[k, b], along_t(b)).wait_recv()

            i = mine(k)
            r1[k, t] = s1[k, i]
            for half in range(2):
                lanes = slice(128 * half, 128 * half + 128)
                for a, v in enumerate(butterfly([r1[k, b, :, lanes].astype(F32) for b in range(NT)])):
                    s2[k, a, :, lanes] = v.astype(BF16)

            @pl.loop(1, NT)
            def _(o):
                second(k, (t + o) % NT).start()

            wbuf[k, pl.ds(pl.multiple_of(y * SLICE + i * TILE, 16), TILE), :] = s2[k, t]

    def direct_out(b):
        return rcopy(acs.at[b], a1.at[t], a1s.at[b], a1r.at[t], along_t(b))

    def direct_back(b):
        return rcopy(a2.at[b], a3.at[t], a3s.at[b], a3r.at[t], along_t(b))

    def direct_start():
        @pl.loop(1, NT)
        def _(o):
            direct_out((t + o) % NT).start()

        a1[t] = acs[t]

    def unpack_own():
        for g in get_own:
            g.wait()

        @pl.loop(0, DIRECT // 64)
        def _(blk):
            rows = pl.ds(pl.multiple_of(blk * 64, 64), 64)
            for k, halves in enumerate(unpacked(dbuf[rows, :])):
                for c in range(2):
                    own[k, rows, 128 * c : 128 * c + 128] = halves[c]

    def direct_rotate():
        @pl.loop(1, NT)
        def _(o):
            b = (t + o) % NT
            rcopy(acs.at[0], a1.at[b], a1s.at[0], a1r.at[b], along_t(b)).wait_recv()

        for cut in range(DIRECT // 128):
            lanes = slice(128 * cut, 128 * cut + 128)
            for b, v in enumerate(butterfly([a1[b, :, lanes].astype(F32) for b in range(NT)])):
                a2[b, :, lanes] = v.astype(BF16)

        @pl.loop(1, NT)
        def _(o):
            direct_back((t + o) % NT).start()

        a3[t] = a2[t]

    def swap_direct():
        return rcopy(aces, acer, asem.at[0], asem.at[1], along_t(sib))

    def direct_product():
        @pl.loop(1, NT)
        def _(o):
            b = (t + o) % NT
            rcopy(a2.at[0], a3.at[b], a3s.at[0], a3r.at[b], along_t(b)).wait_recv()

        lhs = a3[...].reshape(ROWS, DIRECT)
        for k in range(CHUNKS):
            v = jnp.dot(lhs, own[k], preferred_element_type=F32)
            aces[k] = jnp.where(core == 0, v[:, 128:], v[:, :128]).astype(BF16)
            pa[k] = jnp.where(core == 0, v[:, :128], v[:, 128:])
        swap_direct().start()

    lane16 = iota((TILE, 128), 1)

    def put_direct(blk, rows, quarters):
        for u in range(2):
            v, w = quarters[2 * u], quarters[2 * u + 1]
            at = 384 * u
            acs[blk, :, at : at + 128] = v[:, :128].astype(BF16)
            acs[blk, :, at + 128 : at + 256] = jnp.where(
                lane16 < 64, v[:, 128:], pltpu.roll(w[:, 128:], 64, 1)
            ).astype(BF16)
            acs[blk, :, at + 256 : at + 384] = w[:, :128].astype(BF16)

    inner(TAKEN, QPAD - TAKEN, put_direct)

    direct_start()
    inr[x] = ins[x]
    unpack_own()

    def assembled(k):
        @pl.loop(0, TILES)
        def _(i):
            @pl.when(owner(k, i) != t)
            def _():
                rcopy(s2.at[k, 0], tile_at(k, i), s2s.at[k, 0], s2r.at[k, i], along_t(owner(k, i))).wait_recv()

    def hop(k, step, sign, away):
        yy = (y - sign * away + NY) % NY
        off, n = 0, SLICE
        if step == 3:
            n = FAR[k % 2 if sign > 0 else 1 - k % 2]
            off = 0 if sign > 0 else SLICE - n
        part = wbuf.at[k, pl.ds(pl.multiple_of(yy * SLICE + off, 16), n)]
        if sign > 0:
            return rcopy(part, part, us.at[k, step], ur.at[k, step], (up, t))
        return rcopy(part, part, ds.at[k, step], dr.at[k, step], (down, t))

    def ring(k, s):
        for sign in (1, -1):
            if s:
                hop(k, s - 1, sign, s).wait_recv()
            if s < 4:
                hop(k, s, sign, s).start()

    def swap_cores(k):
        return rcopy(ces.at[k], cer.at[k], css.at[k], crs.at[k], along_t(sib))

    def partials(k):
        w = wbuf[k]
        for p in range(NX):
            v = jnp.dot(inr[p], w, preferred_element_type=F32)
            ces[k, p] = jnp.where(core == 0, v[:, 128:], v[:, :128]).astype(BF16)
            pk[k, p] = jnp.where(core == 0, v[:, :128], v[:, 128:])
        swap_cores(k).start()

    def over_x(k, p):
        return rcopy(xs.at[k, p], xr.at[k, x], xss.at[k, p], xrs.at[k, x], along_x(p))

    def reduce_x(k):
        swap_cores(k).wait_recv()
        for p in range(NX):
            v = pk[k, p] + cer[k, p].astype(F32)
            pk[k, p] = v
            xs[k, p] = v.astype(BF16)
        for d in (2, 1, 3):
            over_x(k, (x + d) % NX).start()

    def over_z(k, i):
        return rcopy(zs.at[k, i], zr.at[z], zss.at[k, i], zrs.at[z], along_t(2 * (k + 4 * i) + core))

    lane1 = iota((HALF, 128), 1)

    def reduce_z(k):
        for d in (1, 3, 2):
            src = (x + d) % NX
            rcopy(xs.at[k, 0], xr.at[k, src], xss.at[k, 0], xrs.at[k, src], along_x(src)).wait_recv()
        total = pk[k, x] + pa[k] + acer[k].astype(F32)
        for d in (1, 2, 3):
            total = total + xr[k, (x + d) % NX].astype(F32)
        top, low = total[:HALF], total[HALF:]
        packed = (
            jnp.where(lane1 < 64, top, pltpu.roll(low, 64, 1)),
            jnp.where(lane1 < 64, pltpu.roll(top, 64, 1), low),
        )
        for i in range(2):
            zs[k, i] = packed[i].astype(BF16)

            @pl.when(k + 4 * i != z)
            def _():
                over_z(k, i).start()

            @pl.when(k + 4 * i == z)
            def _():
                fs[...] = packed[i]

    assembled(0)
    ring(0, 0)
    assembled(1)
    ring(1, 0)
    assembled(2)
    ring(2, 0)
    ring(0, 1)
    ring(1, 1)
    assembled(3)
    ring(3, 0)
    ring(0, 2)
    ring(2, 1)
    ring(1, 2)
    ring(0, 3)
    ring(3, 1)
    ring(2, 2)
    ring(1, 3)
    direct_rotate()
    for d in (1, 3, 2):
        src = (x + d) % NX
        rcopy(ins.at[0], inr.at[src], iss.at[0], irs.at[src], along_x(src)).wait_recv()
    ring(0, 4)
    partials(0)
    ring(3, 2)
    reduce_x(0)
    ring(2, 3)
    ring(1, 4)
    partials(1)
    ring(3, 3)
    reduce_x(1)
    ring(2, 4)
    partials(2)
    reduce_x(2)
    ring(3, 4)
    partials(3)
    reduce_x(3)
    direct_product()
    swap_direct().wait_recv()
    reduce_z(0)

    for k in range(CHUNKS):

        @pl.loop(0, TILES)
        def _(i):
            @pl.when(owner(k, i) != t)
            def _():
                first(k, i).wait_send()

        @pl.when(mine(k) < TILES)
        def _():
            @pl.loop(1, NT)
            def _(o):
                second(k, (t + o) % NT).wait_send()

    @pl.loop(1, NT)
    def _(o):
        direct_out((t + o) % NT).wait_send()
        direct_back((t + o) % NT).wait_send()

    swap_direct().wait_send()
    for d in (1, 2, 3):
        spread((x + d) % NX).wait_send()
    for k in range(CHUNKS):
        for s in range(4):
            hop(k, s, 1, s).wait_send()
            hop(k, s, -1, s).wait_send()
        swap_cores(k).wait_send()

    reduce_z(1)
    reduce_z(2)
    reduce_z(3)
    for k in range(CHUNKS):
        for d in (1, 2, 3):
            over_x(k, (x + d) % NX).wait_send()

    get_expo.wait()
    lane8 = iota((8, 128), 1)
    e = ebuf[...]
    mpad[0:8, :] = jnp.where(
        (lane8 < 64) == (core == 0), jnp.left_shift(1, e + 16), jnp.left_shift(1, pltpu.roll(e, 64, 1) + 16)
    ).astype(F32)

    def total_of_z(o, acc):
        src = (z + o) % 8
        rcopy(zs.at[0, 0], zr.at[src], zss.at[0, 0], zrs.at[src], along_t(2 * src + core)).wait_recv()
        return acc + zr[src].astype(F32)

    total = lax.fori_loop(1, 8, total_of_z, fs[...])
    total = total * (mpad[pl.ds(z, 1), :] * (2.0 ** -28))
    turned = total.T
    out[:, 0:HALF] = turned[0:64].astype(BF16)
    out[:, HALF:ROWS] = turned[64:128].astype(BF16)
    for k in range(CHUNKS):
        for i in range(2):

            @pl.when(k + 4 * i != z)
            def _():
                over_z(k, i).wait_send()


def per_device(hidden_acts, mixing, packed_codes, exponents):
    vmem = pltpu.VMEM
    dma = pltpu.SemaphoreType.DMA
    scratch = [
        vmem((ROWS, BLOCK), BF16),
        vmem((SLICE, COLS), jnp.int32),
        vmem((DIRECT, COLS), jnp.int32),
        vmem((INNER_M, INNER_M), F32),
        vmem((8, 128), jnp.int32),
        vmem((128, 128), F32),
        vmem((QPAD + 64, QPAD), BF16),
        vmem((4, ROWS, TAKEN), F32),
        vmem((CHUNKS, TILES, TILE, COLS), BF16),
        vmem((CHUNKS, NT, TILE, COLS), BF16),
        vmem((CHUNKS, NT, TILE, COLS), BF16),
        vmem((CHUNKS, TAKEN, COLS), BF16),
        vmem((NX, ROWS, TAKEN), BF16),
        vmem((NX, ROWS, TAKEN), BF16),
        vmem((CHUNKS, NX, ROWS, 128), F32),
        vmem((CHUNKS, NX, ROWS, 128), BF16),
        vmem((CHUNKS, NX, ROWS, 128), BF16),
        vmem((CHUNKS, NX, ROWS, 128), BF16),
        vmem((CHUNKS, NX, ROWS, 128), BF16),
        vmem((CHUNKS, 2, HALF, 128), BF16),
        vmem((8, HALF, 128), BF16),
        vmem((HALF, 128), F32),
        vmem((CHUNKS, DIRECT, COLS), BF16),
        vmem((NT, TILE, DIRECT), BF16),
        vmem((NT, TILE, DIRECT), BF16),
        vmem((NT, TILE, DIRECT), BF16),
        vmem((NT, TILE, DIRECT), BF16),
        vmem((CHUNKS, ROWS, 128), F32),
        vmem((CHUNKS, ROWS, 128), BF16),
        vmem((CHUNKS, ROWS, 128), BF16),
        dma((10,)),
        dma((CHUNKS, TILES)), dma((CHUNKS, NT)),
        dma((CHUNKS, NT)), dma((CHUNKS, TILES)),
        dma((CHUNKS, 4)), dma((CHUNKS, 4)), dma((CHUNKS, 4)), dma((CHUNKS, 4)),
        dma((NX,)), dma((NX,)),
        dma((CHUNKS,)), dma((CHUNKS,)),
        dma((CHUNKS, NX)), dma((CHUNKS, NX)),
        dma((CHUNKS, 2)), dma((8,)),
        dma((NT,)), dma((NT,)), dma((NT,)), dma((NT,)), dma((2,)),
    ]
    in_hbm, in_vmem = pl.BlockSpec(memory_space=pltpu.HBM), pl.BlockSpec(memory_space=pltpu.VMEM)
    return pl.pallas_call(
        kernel,
        out_shape=jax.ShapeDtypeStruct((64, ROWS), BF16),
        in_specs=[in_hbm] * 4,
        out_specs=in_vmem,
        scratch_shapes=scratch,
        compiler_params=pltpu.CompilerParams(
            collective_id=0, has_side_effects=True, vmem_limit_bytes=62 * 2**20
        ),
        name="rotated_projection",
    )(hidden_acts, mixing, packed_codes, exponents.reshape(8, 128)).T


def solution(mesh):
    placed = (P("dp", "tensor"), P(), P("tensor", None), P())
    return jax.shard_map(
        per_device, mesh=mesh, in_specs=placed, out_specs=P("dp", "tensor"), check_vma=False
    )
```

```python
import jax
import jax.numpy as jnp
from jax import lax
from jax.experimental import pallas as pl
from jax.experimental.pallas import tpu as pltpu
from jax.sharding import PartitionSpec as P

MESH = pl.DeviceIdType.MESH
NY, NX, NT = 8, 4, 16
ROWS = 256
HALF = ROWS // 2
INNER_M = 52
BLOCK = 3328
QUARTER = 832
QPAD = 896
TAKEN = 640
REST = QUARTER - TAKEN
DIRECT = 4 * REST
SLICE = TAKEN // NY
TILE = 16
TILES = SLICE // TILE
CHUNKS = 4
COLS = 256
FAR = 48, 32
F32, BF16 = jnp.float32, jnp.bfloat16


def iota(shape, dim):
    return lax.broadcasted_iota(jnp.int32, shape, dim)


def kernel(
    acts, mix, codes, expo, out,
    xbuf, cbuf, dbuf, mixv, ebuf, mpad, gbuf, zbuf, s1, r1, s2, wbuf, ins, inr, pk, ces, cer, xs, xr, zs, zr, fs,
    own, acs, a1, a2, a3, pa, aces, acer,
    lsem, s1s, s1r, s2s, s2r, us, ur, ds, dr, iss, irs, css, crs, xss, xrs, zss, zrs, a1s, a1r, a3s, a3r, asem,
):
    dp = lax.axis_index("dp")
    t = lax.axis_index("tensor")
    y, x = dp // NX, dp % NX
    z, core = t // 2, t % 2
    sib = t + 1 - 2 * core
    up = ((y + 1) % NY) * NX + x
    down = ((y + NY - 1) % NY) * NX + x

    def along_t(dest):
        return (dp, dest)

    def along_x(dest):
        return (y * NX + dest, t)

    def rcopy(src, dst, ssem, rsem, dev):
        return pltpu.make_async_remote_copy(
            src_ref=src, dst_ref=dst, send_sem=ssem, recv_sem=rsem, device_id=dev, device_id_type=MESH
        )

    row0 = pl.multiple_of(x * QUARTER + y * SLICE, 16)
    get_codes = pltpu.make_async_copy(codes.at[pl.ds(row0, SLICE)], cbuf, lsem.at[0])
    get_acts = pltpu.make_async_copy(acts, xbuf, lsem.at[1])
    get_mix = pltpu.make_async_copy(mix, mixv, lsem.at[2])
    get_expo = pltpu.make_async_copy(expo, ebuf, lsem.at[3])
    def all_of(ref, ssem, rsem):
        return rcopy(ref, ref, ssem, rsem, along_t(sib))

    get_own = []
    for u in range(2):
        for at, row, n in (
            (0, 2 * u * QUARTER + TAKEN, 192),
            (192, (2 * u + 1) * QUARTER + TAKEN + 128, 64),
            (256, (2 * u + 1) * QUARTER + TAKEN, 128),
        ):
            get_own.append(pltpu.make_async_copy(
                codes.at[pl.ds(row, n)], dbuf.at[pl.ds(384 * u + at, n)], lsem.at[4 + len(get_own)]
            ))
    get_codes.start()

    barrier = pltpu.get_barrier_semaphore()

    def greet(dev):
        pl.semaphore_signal(barrier, inc=1, device_id=dev, device_id_type=MESH)

    for o in range(1, NT):
        greet(along_t((t + o) % NT))
    for o in range(1, NX):
        greet(along_x((x + o) % NX))
    greet((up, t))
    greet((down, t))

    get_mix.start()
    get_acts.start()
    get_expo.start()
    for g in get_own:
        g.start()
    get_codes.wait()

    def unpacked(words):
        lane = iota((words.shape[0], 128), 1)
        fields = [jnp.right_shift(jnp.left_shift(words, 28 - 4 * f), 28).astype(F32) for f in range(4)]
        for k in range(CHUNKS):
            half = slice(128 * (k % 2), 128 * (k % 2) + 128)
            left, right = fields[k // 2][:, half], fields[k // 2 + 2][:, half]
            yield (
                jnp.where(lane < 64, left, pltpu.roll(right, 64, 1)).astype(BF16),
                jnp.where(lane < 64, pltpu.roll(left, 64, 1), right).astype(BF16),
            )

    for k, halves in enumerate(unpacked(cbuf[...])):
        for c in range(2):
            s1[k, :, :, 128 * c : 128 * c + 128] = halves[c].reshape(TILES, TILE, 128)
    mpad[...] = jnp.zeros_like(mpad)
    get_mix.wait()
    mpad[0:INNER_M, 0:INNER_M] = mixv[...]

    def block_of(v):
        return jnp.right_shift(v * 1261, 16)

    both = jnp.bitwise_and(iota((128, 128), 0), iota((128, 128), 1))
    both = jnp.bitwise_xor(both, jnp.right_shift(both, 2))
    both = jnp.bitwise_xor(both, jnp.right_shift(both, 1))
    had = (1 - 2 * jnp.bitwise_and(both, 1)).astype(F32).astype(BF16)
    cols = iota((128, QPAD), 1)
    inside = cols < QUARTER
    cblock = block_of(cols)
    which = iota((128, QPAD), 0)
    col_block = jnp.where(inside & (cblock == which), 1.0, 0.0).astype(BF16)
    col_inner = jnp.where(inside & (cols - INNER_M * cblock == which), 1.0, 0.0).astype(BF16)
    mixing = mpad[...].astype(BF16)
    right_m = jnp.dot(mixing, col_inner, preferred_element_type=F32).astype(BF16)
    right_h = jnp.dot(had, col_block, preferred_element_type=F32).astype(BF16)

    @pl.loop(0, 4)
    def _(blk):
        at = pl.multiple_of(blk * 240, 16)
        rows = iota((240, 128), 0) + (at - 64)
        ok = (rows >= 0) & (rows < QUARTER)
        rblock = block_of(rows)
        lane = iota((240, 128), 1)
        row_block = jnp.where(ok & (rblock == lane), 1.0, 0.0).astype(BF16)
        row_inner = jnp.where(ok & (rows - INNER_M * rblock == lane), 1.0, 0.0).astype(BF16)
        m_part = jnp.dot(row_inner, right_m, preferred_element_type=F32)
        h_part = jnp.dot(row_block, right_h, preferred_element_type=F32)
        gbuf[pl.ds(at, 240)] = (m_part * h_part).astype(BF16)

    pl.semaphore_wait(barrier, NT - 1 + NX - 1 + 2)

    def owner(k, i):
        return (TILES * k + i) % NT

    def first(k, i):
        return rcopy(s1.at[k, i], r1.at[k, t], s1s.at[k], s1r.at[k], along_t(owner(k, i)))

    for k in range(CHUNKS):

        @pl.loop(0, TILES)
        def _(o):
            i = (t + o) % TILES

            @pl.when(owner(k, i) != t)
            def _():
                first(k, i).start()

    get_acts.wait()

    def spread(q):
        return rcopy(ins.at[q], inr.at[x], iss, irs, along_x(q))

    def inner(lo, n, put):
        for q in range(4):
            at = q * QUARTER - 64 * (q % 2)
            g = gbuf[0:QPAD, lo : lo + n] if q % 2 else gbuf[64 : 64 + QPAD, lo : lo + n]
            zbuf[q, :, 0:n] = jnp.dot(xbuf[:, at : at + QPAD], g, preferred_element_type=F32)

        @pl.loop(0, ROWS // 16)
        def _(blk):
            rows = pl.ds(pl.multiple_of(blk * 16, 16), 16)
            z0, z1, z2, z3 = (zbuf[q, rows, 0:n] for q in range(4))
            u0, u1, u2, u3 = z0 + z1, z0 - z1, z2 + z3, z2 - z3
            put(blk, rows, [v * 0.125 for v in (u0 + u2, u1 + u3, u0 - u2, u1 - u3)])

    def put_taken(blk, rows, quarters):
        for q, v in enumerate(quarters):
            ins[q, rows, :] = v.astype(BF16)

    inner(0, TAKEN, put_taken)
    for d in (2, 1, 3):
        spread((x + d) % NX).start()

    def tile_at(k, i):
        return wbuf.at[k, pl.ds(pl.multiple_of(y * SLICE + i * TILE, 16), TILE)]

    def mine(k):
        return (t + 4 * NT - TILES * k) % NT

    def second(k, a):
        i = mine(k)
        return rcopy(s2.at[k, a], tile_at(k, i), s2s.at[k], s2r.at[k], along_t(a))

    def butterfly(v):
        for bit in (1, 2, 4, 8):
            v = [v[a ^ bit] - v[a] if a & bit else v[a] + v[a ^ bit] for a in range(NT)]
        return v

    for k in range(CHUNKS):

        @pl.when(mine(k) < TILES)
        def _():
            all_of(r1.at[k, pl.ds(0, NT - 1)], s1s.at[k], s1r.at[k]).wait_recv()

            i = mine(k)
            r1[k, t] = s1[k, i]
            for half in range(2):
                lanes = slice(128 * half, 128 * half + 128)
                for a, v in enumerate(butterfly([r1[k, b, :, lanes].astype(F32) for b in range(NT)])):
                    s2[k, a, :, lanes] = v.astype(BF16)

            @pl.loop(1, NT)
            def _(o):
                second(k, (t + o) % NT).start()

            wbuf[k, pl.ds(pl.multiple_of(y * SLICE + i * TILE, 16), TILE), :] = s2[k, t]

    def direct_out(b):
        return rcopy(acs.at[b], a1.at[t], a1s, a1r, along_t(b))

    def direct_back(b):
        return rcopy(a2.at[b], a3.at[t], a3s, a3r, along_t(b))

    def direct_start():
        @pl.loop(1, NT)
        def _(o):
            direct_out((t + o) % NT).start()

        a1[t] = acs[t]

    def unpack_own():
        for g in get_own:
            g.wait()

        @pl.loop(0, DIRECT // 64)
        def _(blk):
            rows = pl.ds(pl.multiple_of(blk * 64, 64), 64)
            for k, halves in enumerate(unpacked(dbuf[rows, :])):
                for c in range(2):
                    own[k, rows, 128 * c : 128 * c + 128] = halves[c]

    def direct_rotate():
        all_of(a1.at[pl.ds(0, NT - 1)], a1s, a1r).wait_recv()

        for cut in range(DIRECT // 128):
            lanes = slice(128 * cut, 128 * cut + 128)
            for b, v in enumerate(butterfly([a1[b, :, lanes].astype(F32) for b in range(NT)])):
                a2[b, :, lanes] = v.astype(BF16)

        @pl.loop(1, NT)
        def _(o):
            direct_back((t + o) % NT).start()

        a3[t] = a2[t]

    def swap_direct():
        return rcopy(aces, acer, asem.at[0], asem.at[1], along_t(sib))

    def direct_product():
        all_of(a3.at[pl.ds(0, NT - 1)], a3s, a3r).wait_recv()

        lhs = a3[...].reshape(ROWS, DIRECT)
        for k in range(CHUNKS):
            v = jnp.dot(lhs, own[k], preferred_element_type=F32)
            aces[k] = jnp.where(core == 0, v[:, 128:], v[:, :128]).astype(BF16)
            pa[k] = jnp.where(core == 0, v[:, :128], v[:, 128:])
        swap_direct().start()

    lane16 = iota((TILE, 128), 1)

    def put_direct(blk, rows, quarters):
        for u in range(2):
            v, w = quarters[2 * u], quarters[2 * u + 1]
            at = 384 * u
            acs[blk, :, at : at + 128] = v[:, :128].astype(BF16)
            acs[blk, :, at + 128 : at + 256] = jnp.where(
                lane16 < 64, v[:, 128:], pltpu.roll(w[:, 128:], 64, 1)
            ).astype(BF16)
            acs[blk, :, at + 256 : at + 384] = w[:, :128].astype(BF16)

    inner(TAKEN, QPAD - TAKEN, put_direct)

    direct_start()
    inr[x] = ins[x]
    unpack_own()

    def assembled(k):
        here = pl.multiple_of(y * SLICE, 16)

        @pl.when(mine(k) < TILES)
        def _():
            all_of(wbuf.at[k, pl.ds(here, SLICE - TILE)], s2s.at[k], s2r.at[k]).wait_recv()

        @pl.when(mine(k) >= TILES)
        def _():
            all_of(wbuf.at[k, pl.ds(here, SLICE)], s2s.at[k], s2r.at[k]).wait_recv()

    def hop(k, step, sign, away):
        yy = (y - sign * away + NY) % NY
        off, n = 0, SLICE
        if step == 3:
            n = FAR[k % 2 if sign > 0 else 1 - k % 2]
            off = 0 if sign > 0 else SLICE - n
        part = wbuf.at[k, pl.ds(pl.multiple_of(yy * SLICE + off, 16), n)]
        if sign > 0:
            return rcopy(part, part, us.at[k], ur.at[k, step], (up, t))
        return rcopy(part, part, ds.at[k], dr.at[k, step], (down, t))

    def ring(k, s):
        for sign in (1, -1):
            if s:
                hop(k, s - 1, sign, s).wait_recv()
            if s < 4:
                hop(k, s, sign, s).start()

    def swap_cores(k):
        return rcopy(ces.at[k], cer.at[k], css.at[k], crs.at[k], along_t(sib))

    def partials(k):
        w = wbuf[k]
        for p in range(NX):
            v = jnp.dot(inr[p], w, preferred_element_type=F32)
            ces[k, p] = jnp.where(core == 0, v[:, 128:], v[:, :128]).astype(BF16)
            pk[k, p] = jnp.where(core == 0, v[:, :128], v[:, 128:])
        swap_cores(k).start()

    def over_x(k, p):
        return rcopy(xs.at[k, p], xr.at[k, x], xss.at[k], xrs.at[k], along_x(p))

    def reduce_x(k):
        swap_cores(k).wait_recv()
        for p in range(NX):
            v = pk[k, p] + cer[k, p].astype(F32)
            pk[k, p] = v
            xs[k, p] = v.astype(BF16)
        for d in (2, 1, 3):
            over_x(k, (x + d) % NX).start()

    def over_z(k, i):
        return rcopy(zs.at[k, i], zr.at[z], zss.at[k, i], zrs, along_t(2 * (k + 4 * i) + core))

    lane1 = iota((HALF, 128), 1)

    def reduce_z(k):
        all_of(xr.at[k, pl.ds(0, NX - 1)], xss.at[k], xrs.at[k]).wait_recv()
        total = pk[k, x] + pa[k] + acer[k].astype(F32)
        for d in (1, 2, 3):
            total = total + xr[k, (x + d) % NX].astype(F32)
        top, low = total[:HALF], total[HALF:]
        packed = (
            jnp.where(lane1 < 64, top, pltpu.roll(low, 64, 1)),
            jnp.where(lane1 < 64, pltpu.roll(top, 64, 1), low),
        )
        for i in range(2):
            zs[k, i] = packed[i].astype(BF16)

            @pl.when(k + 4 * i != z)
            def _():
                over_z(k, i).start()

            @pl.when(k + 4 * i == z)
            def _():
                fs[...] = packed[i]

    assembled(0)
    ring(0, 0)
    assembled(1)
    ring(1, 0)
    assembled(2)
    ring(2, 0)
    ring(0, 1)
    ring(1, 1)
    assembled(3)
    ring(3, 0)
    ring(0, 2)
    ring(2, 1)
    ring(1, 2)
    ring(0, 3)
    ring(3, 1)
    ring(2, 2)
    ring(1, 3)
    direct_rotate()
    all_of(inr.at[pl.ds(0, NX - 1)], iss, irs).wait_recv()
    ring(0, 4)
    partials(0)
    ring(3, 2)
    reduce_x(0)
    ring(2, 3)
    ring(1, 4)
    partials(1)
    ring(3, 3)
    reduce_x(1)
    ring(2, 4)
    partials(2)
    reduce_x(2)
    ring(3, 4)
    partials(3)
    reduce_x(3)
    direct_product()
    swap_direct().wait_recv()
    reduce_z(0)

    for k in range(CHUNKS):

        @pl.when(mine(k) < TILES)
        def _():
            all_of(s1.at[k, pl.ds(0, TILES - 1)], s1s.at[k], s1r.at[k]).wait_send()
            all_of(s2.at[k, pl.ds(0, NT - 1)], s2s.at[k], s2r.at[k]).wait_send()

        @pl.when(mine(k) >= TILES)
        def _():
            all_of(s1.at[k], s1s.at[k], s1r.at[k]).wait_send()

        for sign, (ssem, rsem) in ((1, (us, ur)), (-1, (ds, dr))):
            n = 3 * SLICE + FAR[k % 2 if sign > 0 else 1 - k % 2]
            all_of(wbuf.at[k, pl.ds(0, n)], ssem.at[k], rsem.at[k, 0]).wait_send()
        swap_cores(k).wait_send()

    all_of(acs.at[pl.ds(0, NT - 1)], a1s, a1r).wait_send()
    all_of(ins.at[pl.ds(0, NX - 1)], iss, irs).wait_send()

    reduce_z(1)
    reduce_z(2)
    reduce_z(3)
    all_of(a2.at[pl.ds(0, NT - 1)], a3s, a3r).wait_send()
    swap_direct().wait_send()
    for k in range(CHUNKS):
        all_of(xs.at[k, pl.ds(0, NX - 1)], xss.at[k], xrs.at[k]).wait_send()

    get_expo.wait()
    lane8 = iota((8, 128), 1)
    e = ebuf[...]
    mpad[0:8, :] = jnp.where(
        (lane8 < 64) == (core == 0), jnp.left_shift(1, e + 16), jnp.left_shift(1, pltpu.roll(e, 64, 1) + 16)
    ).astype(F32)

    all_of(zr.at[pl.ds(0, 7)], zss.at[0, 0], zrs).wait_recv()
    total = lax.fori_loop(1, 8, lambda o, acc: acc + zr[(z + o) % 8].astype(F32), fs[...])
    total = total * (mpad[pl.ds(z, 1), :] * (2.0 ** -28))
    turned = total.T
    out[:, 0:HALF] = turned[0:64].astype(BF16)
    out[:, HALF:ROWS] = turned[64:128].astype(BF16)
    for k in range(CHUNKS):
        for i in range(2):

            @pl.when(k + 4 * i != z)
            def _():
                over_z(k, i).wait_send()


def per_device(hidden_acts, mixing, packed_codes, exponents):
    vmem = pltpu.VMEM
    dma = pltpu.SemaphoreType.DMA
    scratch = [
        vmem((ROWS, BLOCK), BF16),
        vmem((SLICE, COLS), jnp.int32),
        vmem((DIRECT, COLS), jnp.int32),
        vmem((INNER_M, INNER_M), F32),
        vmem((8, 128), jnp.int32),
        vmem((128, 128), F32),
        vmem((QPAD + 64, QPAD), BF16),
        vmem((4, ROWS, TAKEN), F32),
        vmem((CHUNKS, TILES, TILE, COLS), BF16),
        vmem((CHUNKS, NT, TILE, COLS), BF16),
        vmem((CHUNKS, NT, TILE, COLS), BF16),
        vmem((CHUNKS, TAKEN, COLS), BF16),
        vmem((NX, ROWS, TAKEN), BF16),
        vmem((NX, ROWS, TAKEN), BF16),
        vmem((CHUNKS, NX, ROWS, 128), F32),
        vmem((CHUNKS, NX, ROWS, 128), BF16),
        vmem((CHUNKS, NX, ROWS, 128), BF16),
        vmem((CHUNKS, NX, ROWS, 128), BF16),
        vmem((CHUNKS, NX, ROWS, 128), BF16),
        vmem((CHUNKS, 2, HALF, 128), BF16),
        vmem((8, HALF, 128), BF16),
        vmem((HALF, 128), F32),
        vmem((CHUNKS, DIRECT, COLS), BF16),
        vmem((NT, TILE, DIRECT), BF16),
        vmem((NT, TILE, DIRECT), BF16),
        vmem((NT, TILE, DIRECT), BF16),
        vmem((NT, TILE, DIRECT), BF16),
        vmem((CHUNKS, ROWS, 128), F32),
        vmem((CHUNKS, ROWS, 128), BF16),
        vmem((CHUNKS, ROWS, 128), BF16),
        dma((10,)),
        dma((CHUNKS,)), dma((CHUNKS,)),
        dma((CHUNKS,)), dma((CHUNKS,)),
        dma((CHUNKS,)), dma((CHUNKS, 4)), dma((CHUNKS,)), dma((CHUNKS, 4)),
        dma(()), dma(()),
        dma((CHUNKS,)), dma((CHUNKS,)),
        dma((CHUNKS,)), dma((CHUNKS,)),
        dma((CHUNKS, 2)), dma(()),
        dma(()), dma(()), dma(()), dma(()), dma((2,)),
    ]
    in_hbm, in_vmem = pl.BlockSpec(memory_space=pltpu.HBM), pl.BlockSpec(memory_space=pltpu.VMEM)
    return pl.pallas_call(
        kernel,
        out_shape=jax.ShapeDtypeStruct((64, ROWS), BF16),
        in_specs=[in_hbm] * 4,
        out_specs=in_vmem,
        scratch_shapes=scratch,
        compiler_params=pltpu.CompilerParams(
            collective_id=0, has_side_effects=True, vmem_limit_bytes=62 * 2**20
        ),
        name="rotated_projection",
    )(hidden_acts, mixing, packed_codes, exponents.reshape(8, 128)).T


def solution(mesh):
    placed = (P("dp", "tensor"), P(), P("tensor", None), P())
    return jax.shard_map(
        per_device, mesh=mesh, in_specs=placed, out_specs=P("dp", "tensor"), check_vma=False
    )
```

```python
import jax
import jax.numpy as jnp
from jax import lax
from jax.experimental import pallas as pl
from jax.experimental.pallas import tpu as pltpu
from jax.sharding import PartitionSpec as P

MESH = pl.DeviceIdType.MESH
NY, NX, NT = 8, 4, 16
ROWS = 256
HALF = ROWS // 2
INNER_M = 52
BLOCK = 3328
QUARTER = 832
QPAD = 896
TAKEN = 640
REST = QUARTER - TAKEN
DIRECT = 4 * REST
SLICE = TAKEN // NY
TILE = 16
TILES = SLICE // TILE
CHUNKS = 4
COLS = 256
FAR = 48, 32
F32, BF16 = jnp.float32, jnp.bfloat16


def iota(shape, dim):
    return lax.broadcasted_iota(jnp.int32, shape, dim)


def kernel(
    acts, mix, codes, expo, out,
    xbuf, cbuf, dbuf, mixv, ebuf, mpad, gbuf, zbuf, s1, r1, s2, wbuf, ins, inr, pk, ces, cer, xs, xr, zs, zr, fs,
    own, acs, a1, a2, a3, pa, aces, acer,
    lsem, s1s, s1r, s2s, s2r, us, ur, ds, dr, iss, irs, css, crs, xss, xrs, zss, zrs, a1s, a1r, a3s, a3r, asem,
):
    dp = lax.axis_index("dp")
    t = lax.axis_index("tensor")
    y, x = dp // NX, dp % NX
    z, core = t // 2, t % 2
    sib = t + 1 - 2 * core
    up = ((y + 1) % NY) * NX + x
    down = ((y + NY - 1) % NY) * NX + x

    def along_t(dest):
        return (dp, dest)

    def along_x(dest):
        return (y * NX + dest, t)

    def rcopy(src, dst, ssem, rsem, dev):
        return pltpu.make_async_remote_copy(
            src_ref=src, dst_ref=dst, send_sem=ssem, recv_sem=rsem, device_id=dev, device_id_type=MESH
        )

    row0 = pl.multiple_of(x * QUARTER + y * SLICE, 16)
    get_codes = pltpu.make_async_copy(codes.at[pl.ds(row0, SLICE)], cbuf, lsem.at[0])
    get_acts = pltpu.make_async_copy(acts, xbuf, lsem.at[1])
    get_mix = pltpu.make_async_copy(mix, mixv, lsem.at[2])
    get_expo = pltpu.make_async_copy(expo, ebuf, lsem.at[3])
    def all_of(ref, ssem, rsem):
        return rcopy(ref, ref, ssem, rsem, along_t(sib))

    get_own = []
    for u in range(2):
        for at, row, n in (
            (0, 2 * u * QUARTER + TAKEN, 192),
            (192, (2 * u + 1) * QUARTER + TAKEN + 128, 64),
            (256, (2 * u + 1) * QUARTER + TAKEN, 128),
        ):
            get_own.append(pltpu.make_async_copy(
                codes.at[pl.ds(row, n)], dbuf.at[pl.ds(384 * u + at, n)], lsem.at[4 + len(get_own)]
            ))
    get_codes.start()

    barrier = pltpu.get_barrier_semaphore()

    def greet(dev):
        pl.semaphore_signal(barrier, inc=1, device_id=dev, device_id_type=MESH)

    for o in range(1, NT):
        greet(along_t((t + o) % NT))
    for o in range(1, NX):
        greet(along_x((x + o) % NX))
    greet((up, t))
    greet((down, t))

    get_mix.start()
    get_acts.start()
    get_expo.start()
    for g in get_own:
        g.start()
    get_codes.wait()

    def unpacked(words):
        lane = iota((words.shape[0], 128), 1)
        fields = [jnp.right_shift(jnp.left_shift(words, 28 - 4 * f), 28).astype(F32) for f in range(4)]
        for k in range(CHUNKS):
            half = slice(128 * (k % 2), 128 * (k % 2) + 128)
            left, right = fields[k // 2][:, half], fields[k // 2 + 2][:, half]
            yield (
                jnp.where(lane < 64, left, pltpu.roll(right, 64, 1)).astype(BF16),
                jnp.where(lane < 64, pltpu.roll(left, 64, 1), right).astype(BF16),
            )

    for k, halves in enumerate(unpacked(cbuf[...])):
        for c in range(2):
            s1[k, :, :, 128 * c : 128 * c + 128] = halves[c].reshape(TILES, TILE, 128)
    mpad[...] = jnp.zeros_like(mpad)
    get_mix.wait()
    mpad[0:INNER_M, 0:INNER_M] = mixv[...]

    def block_of(v):
        return jnp.right_shift(v * 1261, 16)

    both = jnp.bitwise_and(iota((128, 128), 0), iota((128, 128), 1))
    both = jnp.bitwise_xor(both, jnp.right_shift(both, 2))
    both = jnp.bitwise_xor(both, jnp.right_shift(both, 1))
    had = (1 - 2 * jnp.bitwise_and(both, 1)).astype(F32).astype(BF16)
    cols = iota((128, QPAD), 1)
    inside = cols < QUARTER
    cblock = block_of(cols)
    which = iota((128, QPAD), 0)
    col_block = jnp.where(inside & (cblock == which), 1.0, 0.0).astype(BF16)
    col_inner = jnp.where(inside & (cols - INNER_M * cblock == which), 1.0, 0.0).astype(BF16)
    mixing = mpad[...].astype(BF16)
    right_m = jnp.dot(mixing, col_inner, preferred_element_type=F32).astype(BF16)
    right_h = jnp.dot(had, col_block, preferred_element_type=F32).astype(BF16)

    @pl.loop(0, 4)
    def _(blk):
        at = pl.multiple_of(blk * 240, 16)
        rows = iota((240, 128), 0) + (at - 64)
        ok = (rows >= 0) & (rows < QUARTER)
        rblock = block_of(rows)
        lane = iota((240, 128), 1)
        row_block = jnp.where(ok & (rblock == lane), 1.0, 0.0).astype(BF16)
        row_inner = jnp.where(ok & (rows - INNER_M * rblock == lane), 1.0, 0.0).astype(BF16)
        m_part = jnp.dot(row_inner, right_m, preferred_element_type=F32)
        h_part = jnp.dot(row_block, right_h, preferred_element_type=F32)
        gbuf[pl.ds(at, 240)] = (m_part * h_part).astype(BF16)

    pl.semaphore_wait(barrier, NT - 1 + NX - 1 + 2)

    def owner(k, i):
        return (TILES * k + i) % NT

    def first(k, i):
        return rcopy(s1.at[k, i], r1.at[k, t], s1s.at[k], s1r.at[k], along_t(owner(k, i)))

    for k in range(CHUNKS):

        @pl.loop(0, TILES)
        def _(o):
            i = (t + o) % TILES

            @pl.when(owner(k, i) != t)
            def _():
                first(k, i).start()

    get_acts.wait()

    def spread(q):
        return rcopy(ins.at[q], inr.at[x], iss, irs, along_x(q))

    def inner(lo, n, put):
        for q in range(4):
            at = q * QUARTER - 64 * (q % 2)
            g = gbuf[0:QPAD, lo : lo + n] if q % 2 else gbuf[64 : 64 + QPAD, lo : lo + n]
            zbuf[q, :, 0:n] = jnp.dot(xbuf[:, at : at + QPAD], g, preferred_element_type=F32)

        @pl.loop(0, ROWS // 16)
        def _(blk):
            rows = pl.ds(pl.multiple_of(blk * 16, 16), 16)
            z0, z1, z2, z3 = (zbuf[q, rows, 0:n] for q in range(4))
            u0, u1, u2, u3 = z0 + z1, z0 - z1, z2 + z3, z2 - z3
            put(blk, rows, [v * 0.125 for v in (u0 + u2, u1 + u3, u0 - u2, u1 - u3)])

    def put_taken(blk, rows, quarters):
        for q, v in enumerate(quarters):
            ins[q, rows, :] = v.astype(BF16)

    inner(0, TAKEN, put_taken)
    for d in (2, 1, 3):
        spread((x + d) % NX).start()

    def tile_at(k, i):
        return wbuf.at[k, pl.ds(pl.multiple_of(y * SLICE + i * TILE, 16), TILE)]

    def mine(k):
        return (t + 4 * NT - TILES * k) % NT

    def second(k, a):
        i = mine(k)
        return rcopy(s2.at[k, a], tile_at(k, i), s2s.at[k], s2r.at[k], along_t(a))

    def butterfly(v):
        for bit in (1, 2, 4, 8):
            v = [v[a ^ bit] - v[a] if a & bit else v[a] + v[a ^ bit] for a in range(NT)]
        return v

    for k in range(CHUNKS):

        @pl.when(mine(k) < TILES)
        def _():
            all_of(r1.at[k, pl.ds(0, NT - 1)], s1s.at[k], s1r.at[k]).wait_recv()

            i = mine(k)
            r1[k, t] = s1[k, i]
            for half in range(2):
                lanes = slice(128 * half, 128 * half + 128)
                for a, v in enumerate(butterfly([r1[k, b, :, lanes].astype(F32) for b in range(NT)])):
                    s2[k, a, :, lanes] = v.astype(BF16)

            @pl.loop(1, NT)
            def _(o):
                second(k, (t + o) % NT).start()

            wbuf[k, pl.ds(pl.multiple_of(y * SLICE + i * TILE, 16), TILE), :] = s2[k, t]

    def direct_out(b):
        return rcopy(acs.at[b], a1.at[t], a1s, a1r, along_t(b))

    def direct_back(b):
        return rcopy(a2.at[b], a3.at[t], a3s, a3r, along_t(b))

    def direct_start():
        @pl.loop(1, NT)
        def _(o):
            direct_out((t + o) % NT).start()

        a1[t] = acs[t]

    def unpack_own():
        for g in get_own:
            g.wait()

        @pl.loop(0, DIRECT // 64)
        def _(blk):
            rows = pl.ds(pl.multiple_of(blk * 64, 64), 64)
            for k, halves in enumerate(unpacked(dbuf[rows, :])):
                for c in range(2):
                    own[k, rows, 128 * c : 128 * c + 128] = halves[c]

    def direct_rotate():
        all_of(a1.at[pl.ds(0, NT - 1)], a1s, a1r).wait_recv()

        for cut in range(DIRECT // 128):
            lanes = slice(128 * cut, 128 * cut + 128)
            for b, v in enumerate(butterfly([a1[b, :, lanes].astype(F32) for b in range(NT)])):
                a2[b, :, lanes] = v.astype(BF16)

        @pl.loop(1, NT)
        def _(o):
            direct_back((t + o) % NT).start()

        a3[t] = a2[t]

    def swap_direct():
        return rcopy(aces, acer, asem.at[0], asem.at[1], along_t(sib))

    def direct_product():
        all_of(a3.at[pl.ds(0, NT - 1)], a3s, a3r).wait_recv()

        lhs = a3[...].reshape(ROWS, DIRECT)
        for k in range(CHUNKS):
            v = jnp.dot(lhs, own[k], preferred_element_type=F32)
            aces[k] = jnp.where(core == 0, v[:, 128:], v[:, :128]).astype(BF16)
            pa[k] = jnp.where(core == 0, v[:, :128], v[:, 128:])
        swap_direct().start()

    lane16 = iota((TILE, 128), 1)

    def put_direct(blk, rows, quarters):
        for u in range(2):
            v, w = quarters[2 * u], quarters[2 * u + 1]
            at = 384 * u
            acs[blk, :, at : at + 128] = v[:, :128].astype(BF16)
            acs[blk, :, at + 128 : at + 256] = jnp.where(
                lane16 < 64, v[:, 128:], pltpu.roll(w[:, 128:], 64, 1)
            ).astype(BF16)
            acs[blk, :, at + 256 : at + 384] = w[:, :128].astype(BF16)

    inner(TAKEN, QPAD - TAKEN, put_direct)

    direct_start()
    inr[x] = ins[x]
    unpack_own()

    def assembled(k):
        here = pl.multiple_of(y * SLICE, 16)

        @pl.when(mine(k) < TILES)
        def _():
            all_of(wbuf.at[k, pl.ds(here, SLICE - TILE)], s2s.at[k], s2r.at[k]).wait_recv()

        @pl.when(mine(k) >= TILES)
        def _():
            all_of(wbuf.at[k, pl.ds(here, SLICE)], s2s.at[k], s2r.at[k]).wait_recv()

    def hop(k, step, sign, away):
        yy = (y - sign * away + NY) % NY
        off, n = 0, SLICE
        if step == 3:
            n = FAR[k % 2 if sign > 0 else 1 - k % 2]
            off = 0 if sign > 0 else SLICE - n
        part = wbuf.at[k, pl.ds(pl.multiple_of(yy * SLICE + off, 16), n)]
        if sign > 0:
            return rcopy(part, part, us.at[k], ur.at[k, step], (up, t))
        return rcopy(part, part, ds.at[k], dr.at[k, step], (down, t))

    def ring(k, s):
        for sign in (1, -1):
            if s:
                hop(k, s - 1, sign, s).wait_recv()
            if s < 4:
                hop(k, s, sign, s).start()

    def swap_cores(k):
        return rcopy(ces.at[k], cer.at[k], css.at[k], crs.at[k], along_t(sib))

    def partials(k):
        w = wbuf[k]
        for p in range(NX):
            v = jnp.dot(inr[p], w, preferred_element_type=F32)
            ces[k, p] = jnp.where(core == 0, v[:, 128:], v[:, :128]).astype(BF16)
            pk[k, p] = jnp.where(core == 0, v[:, :128], v[:, 128:])
        swap_cores(k).start()

    def over_x(k, p):
        return rcopy(xs.at[k, p], xr.at[k, x], xss.at[k], xrs.at[k], along_x(p))

    def reduce_x(k):
        swap_cores(k).wait_recv()
        for p in range(NX):
            v = pk[k, p] + cer[k, p].astype(F32)
            pk[k, p] = v
            xs[k, p] = v.astype(BF16)
        for d in (2, 1, 3):
            over_x(k, (x + d) % NX).start()

    def over_z(k, i):
        return rcopy(zs.at[k, i], zr.at[z], zss.at[k, i], zrs, along_t(2 * (k + 4 * i) + core))

    lane1 = iota((HALF, 128), 1)

    def reduce_z(k):
        all_of(xr.at[k, pl.ds(0, NX - 1)], xss.at[k], xrs.at[k]).wait_recv()
        total = pk[k, x] + pa[k] + acer[k].astype(F32)
        for d in (1, 2, 3):
            total = total + xr[k, (x + d) % NX].astype(F32)
        top, low = total[:HALF], total[HALF:]
        packed = (
            jnp.where(lane1 < 64, top, pltpu.roll(low, 64, 1)),
            jnp.where(lane1 < 64, pltpu.roll(top, 64, 1), low),
        )
        for i in range(2):
            zs[k, i] = packed[i].astype(BF16)

            @pl.when(k + 4 * i != z)
            def _():
                over_z(k, i).start()

            @pl.when(k + 4 * i == z)
            def _():
                fs[...] = packed[i]

    assembled(0)
    ring(0, 0)
    assembled(1)
    ring(1, 0)
    assembled(2)
    ring(2, 0)
    assembled(3)
    ring(3, 0)
    ring(0, 1)
    ring(1, 1)
    ring(2, 1)
    ring(0, 2)
    ring(3, 1)
    ring(1, 2)
    ring(2, 2)
    ring(0, 3)
    ring(3, 2)
    ring(1, 3)
    ring(2, 3)
    direct_rotate()
    all_of(inr.at[pl.ds(0, NX - 1)], iss, irs).wait_recv()
    ring(0, 4)
    partials(0)
    ring(3, 3)
    reduce_x(0)
    ring(1, 4)
    partials(1)
    ring(2, 4)
    reduce_x(1)
    partials(2)
    ring(3, 4)
    reduce_x(2)
    partials(3)
    reduce_x(3)
    direct_product()
    swap_direct().wait_recv()
    reduce_z(0)

    for k in range(CHUNKS):

        @pl.when(mine(k) < TILES)
        def _():
            all_of(s1.at[k, pl.ds(0, TILES - 1)], s1s.at[k], s1r.at[k]).wait_send()
            all_of(s2.at[k, pl.ds(0, NT - 1)], s2s.at[k], s2r.at[k]).wait_send()

        @pl.when(mine(k) >= TILES)
        def _():
            all_of(s1.at[k], s1s.at[k], s1r.at[k]).wait_send()

        for sign, (ssem, rsem) in ((1, (us, ur)), (-1, (ds, dr))):
            n = 3 * SLICE + FAR[k % 2 if sign > 0 else 1 - k % 2]
            all_of(wbuf.at[k, pl.ds(0, n)], ssem.at[k], rsem.at[k, 0]).wait_send()
        swap_cores(k).wait_send()

    all_of(acs.at[pl.ds(0, NT - 1)], a1s, a1r).wait_send()
    all_of(ins.at[pl.ds(0, NX - 1)], iss, irs).wait_send()

    reduce_z(1)
    reduce_z(2)
    reduce_z(3)
    all_of(a2.at[pl.ds(0, NT - 1)], a3s, a3r).wait_send()
    swap_direct().wait_send()
    for k in range(CHUNKS):
        all_of(xs.at[k, pl.ds(0, NX - 1)], xss.at[k], xrs.at[k]).wait_send()

    get_expo.wait()
    lane8 = iota((8, 128), 1)
    e = ebuf[...]
    mpad[0:8, :] = jnp.where(
        (lane8 < 64) == (core == 0), jnp.left_shift(1, e + 16), jnp.left_shift(1, pltpu.roll(e, 64, 1) + 16)
    ).astype(F32)

    all_of(zr.at[pl.ds(0, 7)], zss.at[0, 0], zrs).wait_recv()
    total = lax.fori_loop(1, 8, lambda o, acc: acc + zr[(z + o) % 8].astype(F32), fs[...])
    total = total * (mpad[pl.ds(z, 1), :] * (2.0 ** -28))
    turned = total.T
    out[:, 0:HALF] = turned[0:64].astype(BF16)
    out[:, HALF:ROWS] = turned[64:128].astype(BF16)
    for k in range(CHUNKS):
        for i in range(2):

            @pl.when(k + 4 * i != z)
            def _():
                over_z(k, i).wait_send()


def per_device(hidden_acts, mixing, packed_codes, exponents):
    vmem = pltpu.VMEM
    dma = pltpu.SemaphoreType.DMA
    scratch = [
        vmem((ROWS, BLOCK), BF16),
        vmem((SLICE, COLS), jnp.int32),
        vmem((DIRECT, COLS), jnp.int32),
        vmem((INNER_M, INNER_M), F32),
        vmem((8, 128), jnp.int32),
        vmem((128, 128), F32),
        vmem((QPAD + 64, QPAD), BF16),
        vmem((4, ROWS, TAKEN), F32),
        vmem((CHUNKS, TILES, TILE, COLS), BF16),
        vmem((CHUNKS, NT, TILE, COLS), BF16),
        vmem((CHUNKS, NT, TILE, COLS), BF16),
        vmem((CHUNKS, TAKEN, COLS), BF16),
        vmem((NX, ROWS, TAKEN), BF16),
        vmem((NX, ROWS, TAKEN), BF16),
        vmem((CHUNKS, NX, ROWS, 128), F32),
        vmem((CHUNKS, NX, ROWS, 128), BF16),
        vmem((CHUNKS, NX, ROWS, 128), BF16),
        vmem((CHUNKS, NX, ROWS, 128), BF16),
        vmem((CHUNKS, NX, ROWS, 128), BF16),
        vmem((CHUNKS, 2, HALF, 128), BF16),
        vmem((8, HALF, 128), BF16),
        vmem((HALF, 128), F32),
        vmem((CHUNKS, DIRECT, COLS), BF16),
        vmem((NT, TILE, DIRECT), BF16),
        vmem((NT, TILE, DIRECT), BF16),
        vmem((NT, TILE, DIRECT), BF16),
        vmem((NT, TILE, DIRECT), BF16),
        vmem((CHUNKS, ROWS, 128), F32),
        vmem((CHUNKS, ROWS, 128), BF16),
        vmem((CHUNKS, ROWS, 128), BF16),
        dma((10,)),
        dma((CHUNKS,)), dma((CHUNKS,)),
        dma((CHUNKS,)), dma((CHUNKS,)),
        dma((CHUNKS,)), dma((CHUNKS, 4)), dma((CHUNKS,)), dma((CHUNKS, 4)),
        dma(()), dma(()),
        dma((CHUNKS,)), dma((CHUNKS,)),
        dma((CHUNKS,)), dma((CHUNKS,)),
        dma((CHUNKS, 2)), dma(()),
        dma(()), dma(()), dma(()), dma(()), dma((2,)),
    ]
    in_hbm, in_vmem = pl.BlockSpec(memory_space=pltpu.HBM), pl.BlockSpec(memory_space=pltpu.VMEM)
    return pl.pallas_call(
        kernel,
        out_shape=jax.ShapeDtypeStruct((64, ROWS), BF16),
        in_specs=[in_hbm] * 4,
        out_specs=in_vmem,
        scratch_shapes=scratch,
        compiler_params=pltpu.CompilerParams(
            collective_id=0, has_side_effects=True, vmem_limit_bytes=62 * 2**20
        ),
        name="rotated_projection",
    )(hidden_acts, mixing, packed_codes, exponents.reshape(8, 128)).T


def solution(mesh):
    placed = (P("dp", "tensor"), P(), P("tensor", None), P())
    return jax.shard_map(
        per_device, mesh=mesh, in_specs=placed, out_specs=P("dp", "tensor"), check_vma=False
    )
```
